512 devices in a mesh: crop: 8 (over y, core), row: 16 (over z_lo, x), col: 4 (over z_hi).
Axes of the slice: x: 4, y: 4, z: 16 (z_hi: 4, z_lo: 4; z = z_hi * 4 + z_lo), core: 2. Of those that a mesh axis runs over, the one named last changes fastest.
Arguments:
- pair: bfloat16 [4096, 512, 128], P(('crop', 'row'), 'col'), parts along dimension 0, may hold values from -256 to 256
- norm_gain: float32 [128], replicated, may hold values from 0.5 to 1.5
- norm_bias: float32 [128], replicated, may hold values from -3 to 3
- w_gate: bfloat16 [128, 512], replicated, may hold values from -0.5 to 0.5
- w_up: bfloat16 [128, 512], replicated, may hold values from -0.5 to 0.5
- w_down: bfloat16 [512, 128], replicated, may hold values from -0.25 to 0.25
- head_weight: bfloat16 [1024, 64], P('crop'), parts along dimension 0, may hold values from -1 to 1
- head_bias: float32 [64], replicated, may hold values from -4 to 4
- targets: int32 [4096, 512], P(('crop', 'row'), 'col'), parts along dimension 0, may hold values from 0 to 63
- mask: int32 [4096, 512], P(('crop', 'row'), 'col'), parts along dimension 0, may hold values from 0 to 1
Outputs:
- pair_grad: bfloat16 [4096, 512, 128], P(('crop', 'row'), 'col'), parts along dimension 0
- ln_gain_grad: float32 [1024], P('crop'), parts along dimension 0
- ln_bias_grad: float32 [1024], P('crop'), parts along dimension 0
- w_gate_grad: float32 [1024, 512], P('crop'), parts along dimension 0
- w_up_grad: float32 [1024, 512], P('crop'), parts along dimension 0
- w_down_grad: float32 [4096, 128], P('crop'), parts along dimension 0
- head_weight_grad: float32 [1024, 64], P('crop'), parts along dimension 0
- head_bias_grad: float32 [512], P('crop'), parts along dimension 0
The draws below stay inside these ranges and needn't reach their ends.
There are 8 independent parts, one for each index of `crop`. The reference program is written for one: setup_inputs(seed, part) draws one part's arguments, and reference() takes and returns one part's arrays. A program takes and returns all parts, laid end to end along the dimension named above; an argument that names none is the same for every part. Nothing has to cross between parts.
All inputs are finite; a program needn't handle non-finite values.
Results may differ from the reference program's by a relative error of at most 0.02.
Values may be sent and summed in bfloat16 or wider, within the bound.
No kernel may reach another device: no remote copies, remote signals or barrier semaphores. Data moves between devices by JAX's collectives and lax.ppermute only.
A program may use at most 64 MiB of HBM per device.

```python
import jax
import jax.numpy as jnp
from jax import lax

C = 128
FF = 512
NB = 64
L = 512


def head_columns(key):
    key = jax.random.fold_in(key, 11)
    return jax.random.normal(key, (C, NB), jnp.float32) * C ** (-0.5)


def draw_head_weight(key, part):
    return head_columns(key).astype(jnp.bfloat16)


def draw_pair(key, part):
    key = jax.random.fold_in(key, 3)
    base = jnp.clip(jax.random.normal(key, (L, L, C), jnp.float32), -6.0, 6.0)
    return base.astype(jnp.bfloat16)


def draw_mask(key, part):
    key = jax.random.fold_in(key, 5)
    ticket = jax.random.randint(key, (L, L), 0, 4 * L, jnp.int32)
    row_idx = jax.lax.broadcasted_iota(jnp.int32, (L, L), 0)
    return (ticket < L + 3 * row_idx).astype(jnp.int32)


def place_ends(values, rng, low, largest):
    extent = values.shape
    spot = [jax.random.randint(jax.random.fold_in(rng, axis), (), 0, extent[axis]) for axis in range(len(extent))]
    values = values.at[tuple(spot)].set(low)
    longest = extent.index(max(extent))
    spot[longest] = (spot[longest] + 1) % extent[longest]
    return values.at[tuple(spot)].set(largest)


def centred(own_key, dims, spread, most, held_as=jnp.bfloat16):
    return jnp.clip(spread * jax.random.normal(own_key, dims, jnp.float32), -most, most).astype(held_as)


def setup_inputs(seed: int = 0, part: int = 0) -> dict:
    keys = jax.random.split(jax.random.key(seed), 11)
    part_splits = jax.random.split(jax.random.fold_in(keys[10], part), 11)
    pair = draw_pair(jax.random.fold_in(jax.random.fold_in(keys[10], part), 71), part)
    norm_gain = jnp.clip(1.0 + 0.1 * jax.random.normal(keys[1], (C,), jnp.float32), 0.5, 1.5)
    norm_bias = centred(keys[2], (C,), 0.5, 3.0, jnp.float32)
    w_gate = centred(keys[3], (C, FF), C ** -0.5, 0.5)
    w_up = centred(keys[4], (C, FF), C ** -0.5, 0.5)
    w_down = centred(keys[5], (FF, C), FF ** -0.5, 0.25)
    head_weight = draw_head_weight(jax.random.fold_in(jax.random.fold_in(keys[10], part), 71), part)
    head_bias = centred(keys[7], (NB,), 1.0, 4.0, jnp.float32)
    targets = place_ends(jax.random.randint(part_splits[8], (L, L), 0, NB), jax.random.fold_in(part_splits[8], 1), 0, NB - 1).astype(jnp.int32)
    mask = draw_mask(jax.random.fold_in(jax.random.fold_in(keys[10], part), 71), part)
    return {"pair": pair, "norm_gain": norm_gain, "norm_bias": norm_bias, "w_gate": w_gate, "w_up": w_up, "w_down": w_down, "head_weight": head_weight, "head_bias": head_bias, "targets": targets, "mask": mask}


def layer_normalize(input_rows, norm_gain, norm_bias):
    input_float = input_rows.astype(jnp.float32)
    centered_input = lax.optimization_barrier(jnp.mean(input_float, axis=-1, keepdims=True))
    variance = lax.optimization_barrier(jnp.mean(jnp.square(input_float - centered_input), axis=-1, keepdims=True))
    inverse_deviation = lax.rsqrt(variance + 1e-05)
    standardized_input = (input_float - centered_input) * inverse_deviation
    normalized_rows = (standardized_input * norm_gain + norm_bias).astype(jnp.bfloat16)
    return (input_float, standardized_input, inverse_deviation, normalized_rows)

def reference(pair, norm_gain, norm_bias, w_gate, w_up, w_down, head_weight, head_bias, targets, mask):
    total = L * L
    block = min(4096, total)
    count = total // block
    flat = pair.reshape(count, block, C)

    def forward_block(input_rows):
        input_float, standardized_input, inverse_deviation, normalized_rows = layer_normalize(input_rows, norm_gain, norm_bias)
        gate = jnp.dot(normalized_rows, w_gate, preferred_element_type=jnp.float32)
        up = jnp.dot(normalized_rows, w_up, preferred_element_type=jnp.float32)
        hidden = (jax.nn.silu(gate) * up).astype(jnp.bfloat16)
        return (input_float + jnp.dot(hidden, w_down, preferred_element_type=jnp.float32)).astype(jnp.bfloat16)
    updated = lax.map(forward_block, flat).reshape(total, C)
    half = (jnp.dot(updated, head_weight, preferred_element_type=jnp.float32) + head_bias).astype(jnp.bfloat16)
    half = half.reshape(L, L, NB).astype(jnp.float32)
    symmetric = half + jnp.swapaxes(half, 0, 1)
    prob = jnp.exp(jax.nn.log_softmax(symmetric, axis=-1))
    onehot = (targets[..., None] == jnp.arange(NB, dtype=jnp.int32)).astype(jnp.float32)
    term = mask[..., None].astype(jnp.float32) * (prob - onehot)
    half_grad = (term + jnp.swapaxes(term, 0, 1)).astype(jnp.bfloat16).reshape(total, NB)
    head_weight_grad = jnp.dot(updated.T, half_grad, preferred_element_type=jnp.float32) / L
    head_bias_grad = lax.optimization_barrier(jnp.sum(half_grad.astype(jnp.float32), axis=0)) / L
    updated_grad = jnp.dot(half_grad, head_weight.T, preferred_element_type=jnp.float32)

    def backward_block(carry, inputs):
        gain_accumulated, bias_sum, gate_sum, up_sum, down_sum = carry
        input_rows, grad_in = inputs
        input_float, standardized_input, inverse_deviation, normalized_rows = layer_normalize(input_rows, norm_gain, norm_bias)
        gate = jnp.dot(normalized_rows, w_gate, preferred_element_type=jnp.float32)
        up = jnp.dot(normalized_rows, w_up, preferred_element_type=jnp.float32)
        silu_gate = jax.nn.silu(gate)
        hidden = (silu_gate * up).astype(jnp.bfloat16)
        grad_b = grad_in.astype(jnp.bfloat16)
        down_sum = down_sum + jnp.dot(hidden.T, grad_b, preferred_element_type=jnp.float32)
        hidden_grad = jnp.dot(grad_b, w_down.T, preferred_element_type=jnp.float32)
        sigma = jax.nn.sigmoid(gate)
        gate_grad = (hidden_grad * up * sigma * (1.0 + gate * (1.0 - sigma))).astype(jnp.bfloat16)
        up_grad = (hidden_grad * silu_gate).astype(jnp.bfloat16)
        gate_sum = gate_sum + jnp.dot(normalized_rows.T, gate_grad, preferred_element_type=jnp.float32)
        up_sum = up_sum + jnp.dot(normalized_rows.T, up_grad, preferred_element_type=jnp.float32)
        normalized_gradient = jnp.dot(gate_grad, w_gate.T, preferred_element_type=jnp.float32) + jnp.dot(up_grad, w_up.T, preferred_element_type=jnp.float32)
        gain_accumulated = gain_accumulated + lax.optimization_barrier(jnp.sum(normalized_gradient * standardized_input, axis=0))
        bias_sum = bias_sum + lax.optimization_barrier(jnp.sum(normalized_gradient, axis=0))
        scaled_rows = normalized_gradient * norm_gain
        backward_pass = inverse_deviation * (scaled_rows - lax.optimization_barrier(jnp.mean(scaled_rows, axis=-1, keepdims=True)) - standardized_input * lax.optimization_barrier(jnp.mean(scaled_rows * standardized_input, axis=-1, keepdims=True)))
        result = (grad_in + backward_pass).astype(jnp.bfloat16)
        return ((gain_accumulated, bias_sum, gate_sum, up_sum, down_sum), result)
    start = (jnp.zeros((C,), jnp.float32), jnp.zeros((C,), jnp.float32), jnp.zeros((C, FF), jnp.float32), jnp.zeros((C, FF), jnp.float32), jnp.zeros((FF, C), jnp.float32))
    sums, grads = lax.scan(backward_block, start, (flat, updated_grad.reshape(count, block, C)))
    pair_grad = grads.reshape(L, L, C)
    return (pair_grad, sums[0] / L, sums[1] / L, sums[2] / L, sums[3] / L, sums[4] / L, head_weight_grad, head_bias_grad)
```

```python
import functools

import jax
import jax.numpy as jnp
from jax import lax
from jax.experimental import pallas as pl
from jax.experimental.pallas import tpu as pltpu
from jax.sharding import Mesh, PartitionSpec as P

F32 = jnp.float32
BF16 = jnp.bfloat16
C = 128
FF = 512
NB = 64
SIDE = 32
PAIRS = SIDE * SIDE
SUB = 256
STEPS = PAIRS // SUB
ROWS = SUB // SIDE
WIRE = PAIRS // 2 + 16
GROUP = 16
SHARE = 104
PACK = GROUP * SHARE
GRID_AXES = ("z_lo", "x", "z_hi")
VMEM_LIMIT = 56 * 1024 * 1024


def dot(a, b, a_dim, b_dim):
    return lax.dot_general(
        a, b, (((a_dim,), (b_dim,)), ((), ())), preferred_element_type=F32
    )


def normalize(rows, gain, bias):
    mean = jnp.mean(rows, axis=-1, keepdims=True)
    centered = rows - mean
    variance = jnp.mean(centered * centered, axis=-1, keepdims=True)
    rstd = lax.rsqrt(variance + 1e-05)
    xhat = centered * rstd
    return xhat, rstd, (xhat * gain + bias).astype(BF16)


def sigmoid(v):
    return 0.5 * jnp.tanh(0.5 * v) + 0.5


def spread(ref, start, shift):
    lane = lax.broadcasted_iota(jnp.int32, (8, 128), 1)
    out = jnp.zeros((8, 128), F32)
    for u in range(4):
        rows = ref[pl.ds(start + u, 8, stride=4), :]
        rows = pltpu.roll(rows, lax.rem(shift + 32 * u + 128, 128), 1)
        out = jnp.where((lane >= 32 * u) & (lane < 32 * u + 32), rows, out)
    return out


def send_kernel(
    k_ref, pair_ref, gain_ref, bias_ref, w_gu_ref, w_down_ref, head_ref, head_bias_ref,
    targets_ref, mask_ref, wire_ref, half_ref, codes_ref,
):
    gain, bias = gain_ref[...], bias_ref[...]

    def step(n, _):
        rows = pair_ref[pl.ds(n * ROWS, ROWS)].reshape(SUB, C).astype(F32)
        _, _, normed = normalize(rows, gain, bias)
        gate_up = jnp.dot(normed, w_gu_ref[...], preferred_element_type=F32)
        gate, up = gate_up[:, :FF], gate_up[:, FF:]
        hidden = (gate * sigmoid(gate) * up).astype(BF16)
        updated = (rows + jnp.dot(hidden, w_down_ref[...], preferred_element_type=F32)).astype(BF16)
        half_ref[pl.ds(pl.multiple_of(n * SUB, SUB), SUB), :] = (
            jnp.dot(updated, head_ref[...], preferred_element_type=F32) + head_bias_ref[...]
        )
        return 0

    lax.fori_loop(0, STEPS, step, 0)
    lane = lax.broadcasted_iota(jnp.int32, (SIDE, 128), 1)
    for j in range(SIDE // 2):
        low = half_ref[pl.ds(j, SIDE, stride=SIDE), :]
        high = half_ref[pl.ds(SIDE // 2 + j, SIDE, stride=SIDE), :]
        wire_ref[pl.ds(j * SIDE, SIDE), :] = jnp.where(lane < NB, low, high).astype(BF16)
    codes = jnp.concatenate(
        [targets_ref[...].astype(F32), mask_ref[...].astype(F32), jnp.zeros((64, 128), F32)], axis=0
    )
    codes_ref[...] = codes.T
    start = pl.multiple_of(k_ref[0] * SIDE, SIDE)
    wire_ref[pl.ds(PAIRS // 2, 16), :] = jnp.concatenate(
        [spread(codes_ref, start, 0), spread(codes_ref, start, 96)], axis=0
    ).astype(BF16)


def back_kernel(
    first, last, k_ref, pair_ref, gain_ref, bias_ref, w_gu_ref, w_down_ref, head_ref, head_t_ref,
    head_bias_ref, targets_ref, mask_ref, wire_ref, *rest,
):
    if not first:
        acc_gu_in, acc_down_in, acc_head_in, acc_small_in, _ = rest[:5]
        rest = rest[5:]
    if last:
        pack_ref, grad_ref = rest[:2]
        rest = rest[2:]
    else:
        acc_gu_out, acc_down_out, acc_head_out, acc_small_out, grad_ref = rest[:5]
        rest = rest[5:]
    (normed_s, xhat_s, rstd_s, gate_up_s, hidden_s, updated_s, grad_s, gu_grad_s, codes_s, hg_s, gt_s) = rest
    gain, bias = gain_ref[...], bias_ref[...]

    def forward(n, _):
        at = pl.ds(pl.multiple_of(n * SUB, SUB), SUB)
        rows = pair_ref[pl.ds(n * ROWS, ROWS)].reshape(SUB, C).astype(F32)
        xhat, rstd, normed = normalize(rows, gain, bias)
        normed_s[at, :] = normed
        xhat_s[at, :] = xhat
        rstd_s[at, :] = jnp.broadcast_to(rstd, (SUB, C))
        gate_up = jnp.dot(normed, w_gu_ref[...], preferred_element_type=F32)
        gate_up_s[at, :] = gate_up
        gate, up = gate_up[:, :FF], gate_up[:, FF:]
        hidden = (gate * sigmoid(gate) * up).astype(BF16)
        hidden_s[at, :] = hidden
        updated_s[at, :] = (
            rows + jnp.dot(hidden, w_down_ref[...], preferred_element_type=F32)
        ).astype(BF16)
        return 0

    lax.fori_loop(0, STEPS, forward, 0)

    updated = updated_s[...]
    half = (dot(head_t_ref[...], updated, 1, 1) + head_bias_ref[...]).astype(BF16).astype(F32)
    mirror = wire_ref[pl.ds(0, PAIRS // 2), :].astype(F32).T
    symmetric = half + jnp.concatenate([mirror[:NB], mirror[NB:]], axis=1)
    symmetric = symmetric - jnp.max(symmetric, axis=0, keepdims=True)
    exped = jnp.exp(symmetric)
    prob = exped / jnp.sum(exped, axis=0, keepdims=True)
    shift = lax.rem(128 - k_ref[0] * SIDE, 128)
    codes_s[pl.ds(0, SIDE), :] = targets_ref[...].astype(F32)
    codes_s[pl.ds(SIDE, SIDE), :] = mask_ref[...].astype(F32)
    theirs = wire_ref[pl.ds(PAIRS // 2, 16), :].astype(F32)

    def line(rows):
        return jnp.concatenate([rows[r : r + 1] for r in range(8)], axis=1)

    own_target = line(spread(codes_s, 0, shift))
    own_mask = line(spread(codes_s, SIDE, shift))
    their_target, their_mask = line(theirs[:8]), line(theirs[8:])
    level = lax.broadcasted_iota(jnp.int32, (NB, PAIRS), 0).astype(F32)
    half_grad = (
        own_mask * (prob - jnp.where(level == own_target, 1.0, 0.0))
        + their_mask * (prob - jnp.where(level == their_target, 1.0, 0.0))
    ).astype(BF16)
    hg_s[...] = half_grad
    head_bias_sum = jnp.sum(half_grad.astype(F32), axis=1, keepdims=True)
    grad_s[...] = dot(half_grad, head_t_ref[...], 0, 0)
    grad_t = jnp.dot(head_ref[...], half_grad, preferred_element_type=F32).astype(BF16)
    gt_s[...] = grad_t

    def backward(n, carry):
        gain_sum, bias_sum = carry
        at = pl.ds(pl.multiple_of(n * SUB, SUB), SUB)
        grad_in = grad_s[at, :]
        hidden_grad = dot(grad_in.astype(BF16), w_down_ref[...], 1, 1)
        gate, up = gate_up_s[at, :FF], gate_up_s[at, FF:]
        sigma = sigmoid(gate)
        silu = gate * sigma
        gate_grad = (hidden_grad * up * (sigma * (1.0 + gate * (1.0 - sigma)))).astype(BF16)
        up_grad = (hidden_grad * silu).astype(BF16)
        gu_grad_s[at, :FF] = gate_grad
        gu_grad_s[at, FF:] = up_grad
        normed_grad = dot(gu_grad_s[at, :], w_gu_ref[...], 1, 1)
        xhat, rstd = xhat_s[at, :], rstd_s[at, :]
        product = normed_grad * xhat
        gain_sum = gain_sum + jnp.sum(product, axis=0, keepdims=True)
        bias_sum = bias_sum + jnp.sum(normed_grad, axis=0, keepdims=True)
        scaled = normed_grad * gain
        back = rstd * (
            scaled
            - jnp.mean(scaled, axis=-1, keepdims=True)
            - xhat * jnp.mean(product * gain, axis=-1, keepdims=True)
        )
        grad_ref[pl.ds(n * ROWS, ROWS)] = (grad_in + back).astype(BF16).reshape(ROWS, SIDE, C)
        return gain_sum, bias_sum

    gain_sum, bias_sum = lax.fori_loop(
        0, STEPS, backward, (jnp.zeros((1, C), F32), jnp.zeros((1, C), F32))
    )
    head_sum = jnp.dot(hg_s[...], updated_s[...], preferred_element_type=F32)
    down_sum = jnp.dot(gt_s[...], hidden_s[...], preferred_element_type=F32)
    gu_sum = dot(normed_s[...], gu_grad_s[...], 0, 0)
    head_bias_row = jnp.concatenate(
        [jnp.broadcast_to(head_bias_sum, (NB, 128)), jnp.zeros((NB, 128), F32)], axis=0
    ).T[:1]
    small = jnp.concatenate([gain_sum, bias_sum, head_bias_row, jnp.zeros((5, 128), F32)], axis=0)
    if not first:
        gu_sum = gu_sum + acc_gu_in[...]
        down_sum = down_sum + acc_down_in[...]
        head_sum = head_sum + acc_head_in[...]
        small = small + acc_small_in[...]
    if last:
        for b in range(8):
            pack_ref[pl.ds(b * 128, 128), :] = gu_sum[:, b * 128 : b * 128 + 128].astype(BF16)
        for b in range(4):
            pack_ref[pl.ds(1024 + b * 128, 128), :] = down_sum[:, b * 128 : b * 128 + 128].astype(BF16)
        pack_ref[pl.ds(1536, NB), :] = head_sum.astype(BF16)
        tail = jnp.concatenate([small, jnp.zeros((PACK - 1608, 128), F32)], axis=0)
        pack_ref[pl.ds(1600, PACK - 1600), :] = tail.astype(BF16)
    else:
        acc_gu_out[...] = gu_sum
        acc_down_out[...] = down_sum
        acc_head_out[...] = head_sum
        acc_small_out[...] = small


def unpack_kernel(scale, pack_ref, gain_ref, bias_ref, gate_ref, up_ref, down_ref, head_ref, head_bias_ref):
    def block(b):
        return pack_ref[pl.ds(b * 128, 128), :].astype(F32) * scale

    for b in range(4):
        gate_ref[:, b * 128 : b * 128 + 128] = block(b)
        up_ref[:, b * 128 : b * 128 + 128] = block(4 + b)
        down_ref[pl.ds(b * 128, 128), :] = block(8 + b).T
    tail = block(12)
    head_ref[...] = tail.T[:, :NB]
    gain_ref[...] = tail[NB : NB + 1]
    bias_ref[...] = tail[NB + 1 : NB + 2]
    head_bias_ref[...] = tail[NB + 2 : NB + 3]


def full(shape):
    return pl.BlockSpec(shape, lambda i, k: (0,) * len(shape))


def on_device(
    pair, norm_gain, norm_bias, w_gate, w_up, w_down, head_weight, head_bias, targets, mask
):
    length = SIDE * 16
    place = lax.axis_index("x")
    gain, bias = norm_gain[None], norm_bias[None]
    w_gu = jnp.concatenate([w_gate, w_up], axis=1)
    head_t = head_weight.T
    head_twice = jnp.concatenate([head_weight, head_weight], axis=1)
    head_bias_twice = jnp.concatenate([head_bias, head_bias])[None]
    head_bias_column = head_bias[:, None]
    block = pl.BlockSpec((SIDE, SIDE, C), lambda i, k: (0, k[0], 0))
    params = pltpu.CompilerParams(vmem_limit_bytes=VMEM_LIMIT)

    def send(shift):
        k = lax.rem(place + shift, 4)[None]
        wire = pl.pallas_call(
            send_kernel,
            grid_spec=pltpu.PrefetchScalarGridSpec(
                num_scalar_prefetch=1,
                grid=(1,),
                in_specs=[
                    block, full((1, C)), full((1, C)), full((C, 2 * FF)), full((FF, C)),
                    full((C, 2 * NB)), full((1, 2 * NB)), full((SIDE, 128)), full((SIDE, 128)),
                ],
                out_specs=full((WIRE, 128)),
                scratch_shapes=[pltpu.VMEM((PAIRS, 128), F32), pltpu.VMEM((128, 128), F32)],
            ),
            out_shape=jax.ShapeDtypeStruct((WIRE, 128), BF16),
            compiler_params=params,
            cost_estimate=pl.CostEstimate(
                flops=2 * PAIRS * C * 13 * NB * 2, bytes_accessed=1 << 20, transcendentals=PAIRS * FF
            ),
            name="forward_send",
        )(k, pair, gain, bias, w_gu, w_down, head_twice, head_bias_twice, targets, mask)
        route = [
            ((a * 4 + x) * 4 + b, (b * 4 + (x + shift) % 4) * 4 + a)
            for a in range(4) for x in range(4) for b in range(4)
        ]
        return lax.ppermute(wire, GRID_AXES, route)

    wires = [send(shift) for shift in range(4)]
    sums = [
        jax.ShapeDtypeStruct((C, 2 * FF), F32),
        jax.ShapeDtypeStruct((C, FF), F32),
        jax.ShapeDtypeStruct((NB, C), F32),
        jax.ShapeDtypeStruct((8, C), F32),
    ]
    sum_specs = [full(s.shape) for s in sums]
    state = ()
    for shift in range(4):
        first, last = shift == 0, shift == 3
        k = lax.rem(place + (4 - shift), 4)[None]
        out_shape = [jax.ShapeDtypeStruct((PACK, 128), BF16)] if last else list(sums)
        out_specs = [full((PACK, 128))] if last else list(sum_specs)
        aliases = {}
        if not first:
            aliases[12 + 4] = len(out_shape)
            if not last:
                aliases.update({12 + n: n for n in range(4)})
        state = pl.pallas_call(
            functools.partial(back_kernel, first, last),
            grid_spec=pltpu.PrefetchScalarGridSpec(
                num_scalar_prefetch=1,
                grid=(1,),
                in_specs=[
                    block, full((1, C)), full((1, C)), full((C, 2 * FF)), full((FF, C)),
                    full((C, NB)), full((NB, C)), full((NB, 1)), full((SIDE, 128)), full((SIDE, 128)),
                    full((WIRE, 128)),
                ] + ([] if first else sum_specs + [pl.BlockSpec(memory_space=pl.ANY)]),
                out_specs=out_specs + [block],
                scratch_shapes=[
                    pltpu.VMEM((PAIRS, C), BF16),
                    pltpu.VMEM((PAIRS, C), F32),
                    pltpu.VMEM((PAIRS, C), F32),
                    pltpu.VMEM((PAIRS, 2 * FF), F32),
                    pltpu.VMEM((PAIRS, FF), BF16),
                    pltpu.VMEM((PAIRS, C), BF16),
                    pltpu.VMEM((PAIRS, C), F32),
                    pltpu.VMEM((PAIRS, 2 * FF), BF16),
                    pltpu.VMEM((2 * SIDE, 128), F32),
                    pltpu.VMEM((NB, PAIRS), BF16),
                    pltpu.VMEM((C, PAIRS), BF16),
                ],
            ),
            out_shape=out_shape + [jax.ShapeDtypeStruct(pair.shape, BF16)],
            input_output_aliases=aliases,
            compiler_params=params,
            cost_estimate=pl.CostEstimate(
                flops=2 * PAIRS * C * FF * 11, bytes_accessed=1 << 21, transcendentals=PAIRS * FF
            ),
            name="backward_block",
        )(
            k, pair, gain, bias, w_gu, w_down, head_weight, head_t, head_bias_column, targets, mask,
            wires[shift], *state,
        )
    pack, pair_grad = state

    spread_out = lax.all_to_all(pack.reshape(GROUP, SHARE, 128), ("z_lo", "x"), 0, 0)
    share = jnp.sum(spread_out.astype(F32), axis=0).astype(BF16)
    shares = lax.all_to_all(jnp.broadcast_to(share, (4, SHARE, 128)), "z_hi", 0, 0)
    share = jnp.sum(shares.astype(F32), axis=0).astype(BF16)
    pack = lax.all_to_all(
        jnp.broadcast_to(share, (GROUP, SHARE, 128)), ("z_lo", "x"), 0, 0
    ).reshape(PACK, 128)

    outs = pl.pallas_call(
        functools.partial(unpack_kernel, 1.0 / length),
        out_shape=[
            jax.ShapeDtypeStruct((1, C), F32),
            jax.ShapeDtypeStruct((1, C), F32),
            jax.ShapeDtypeStruct((C, FF), F32),
            jax.ShapeDtypeStruct((C, FF), F32),
            jax.ShapeDtypeStruct((FF, C), F32),
            jax.ShapeDtypeStruct((C, NB), F32),
            jax.ShapeDtypeStruct((1, 128), F32),
        ],
        compiler_params=params,
        name="unpack_sums",
    )(pack)
    gain_tot, bias_tot, gate_tot, up_tot, down_tot, head_tot, head_bias_tot = outs
    return (
        pair_grad, gain_tot[0], bias_tot[0], gate_tot, up_tot, down_tot, head_tot,
        head_bias_tot[0, :NB],
    )


def solution(mesh):
    fine = Mesh(mesh.devices.reshape(8, 4, 4, 4), ("crop",) + GRID_AXES)
    rows = ("crop", "z_lo", "x")
    in_specs = (
        P(rows, "z_hi", None), P(), P(), P(), P(), P(), P("crop", None), P(),
        P(rows, "z_hi"), P(rows, "z_hi"),
    )
    out_specs = (
        P(rows, "z_hi", None), P("crop"), P("crop"), P("crop", None), P("crop", None),
        P("crop", None), P("crop", None), P("crop"),
    )
    return jax.shard_map(
        on_device, mesh=fine, in_specs=in_specs, out_specs=out_specs, check_vma=False
    )
```

```python
import functools

import jax
import jax.numpy as jnp
from jax import lax
from jax.experimental import pallas as pl
from jax.experimental.pallas import tpu as pltpu
from jax.sharding import Mesh, PartitionSpec as P

F32 = jnp.float32
BF16 = jnp.bfloat16
C = 128
FF = 512
NB = 64
SIDE = 32
PAIRS = SIDE * SIDE
SUB = PAIRS
STEPS = PAIRS // SUB
ROWS = SUB // SIDE
WIRE = PAIRS // 2 + 16
GROUP = 16
SHARE = 104
PACK = GROUP * SHARE
GRID_AXES = ("z_lo", "x", "z_hi")
VMEM_LIMIT = 56 * 1024 * 1024


def dot(a, b, a_dim, b_dim):
    return lax.dot_general(
        a, b, (((a_dim,), (b_dim,)), ((), ())), preferred_element_type=F32
    )


def normalize(rows, gain, bias):
    mean = jnp.mean(rows, axis=-1, keepdims=True)
    centered = rows - mean
    variance = jnp.mean(centered * centered, axis=-1, keepdims=True)
    rstd = lax.rsqrt(variance + 1e-05)
    xhat = centered * rstd
    return xhat, rstd, (xhat * gain + bias).astype(BF16)


def sigmoid(v):
    return 0.5 * jnp.tanh(0.5 * v) + 0.5


def spread(ref, start, shift):
    lane = lax.broadcasted_iota(jnp.int32, (8, 128), 1)
    out = jnp.zeros((8, 128), F32)
    for u in range(4):
        rows = ref[pl.ds(start + u, 8, stride=4), :]
        rows = pltpu.roll(rows, lax.rem(shift + 32 * u + 128, 128), 1)
        out = jnp.where((lane >= 32 * u) & (lane < 32 * u + 32), rows, out)
    return out


def send_kernel(
    k_ref, pair_ref, gain_ref, bias_ref, w_gate_ref, w_up_ref, w_down_ref, head_t_ref, head_bias_ref,
    targets_ref, mask_ref, *rest,
):
    wire_refs, (w_gu_ref, half_ref, codes_ref) = rest[:2], rest[2:]
    turn = pl.program_id(0)

    @pl.when(turn == 0)
    def _():
        w_gu_ref[:, :FF] = w_gate_ref[...]
        w_gu_ref[:, FF:] = w_up_ref[...]
        codes = jnp.concatenate(
            [targets_ref[...].astype(F32), mask_ref[...].astype(F32), jnp.zeros((64, 128), F32)],
            axis=0,
        )
        codes_ref[...] = codes.T

    head_twice = jnp.concatenate([head_t_ref[...], head_t_ref[...]], axis=0)
    head_bias = jnp.concatenate([head_bias_ref[...], head_bias_ref[...]], axis=1)
    rows = pair_ref[...].reshape(PAIRS, C).astype(F32)
    _, _, normed = normalize(rows, gain_ref[...], bias_ref[...])
    gate_up = jnp.dot(normed, w_gu_ref[...], preferred_element_type=F32)
    gate, up = gate_up[:, :FF], gate_up[:, FF:]
    hidden = (gate * sigmoid(gate) * up).astype(BF16)
    updated = (rows + jnp.dot(hidden, w_down_ref[...], preferred_element_type=F32)).astype(BF16)
    half_ref[...] = dot(updated, head_twice, 1, 1) + head_bias
    lane = lax.broadcasted_iota(jnp.int32, (SIDE, 128), 1)
    start = pl.multiple_of(k_ref[turn] * SIDE, SIDE)

    def write(wire_ref):
        for j in range(SIDE // 2):
            low = half_ref[pl.ds(j, SIDE, stride=SIDE), :]
            high = half_ref[pl.ds(SIDE // 2 + j, SIDE, stride=SIDE), :]
            wire_ref[pl.ds(j * SIDE, SIDE), :] = jnp.where(lane < NB, low, high).astype(BF16)
        wire_ref[pl.ds(PAIRS // 2, 16), :] = jnp.concatenate(
            [spread(codes_ref, start, 0), spread(codes_ref, start, 96)], axis=0
        ).astype(BF16)

    for n in range(2):
        pl.when(turn == n)(functools.partial(write, wire_refs[n]))


def back_kernel(
    first, k_ref, pair_ref, gain_ref, bias_ref, w_gate_ref, w_up_ref, w_down_ref, head_t_ref,
    head_bias_ref, targets_ref, mask_ref, wire_a_ref, wire_b_ref, *rest,
):
    turn = pl.program_id(0)
    if first:
        *acc_outs, grad_ref = rest[:5]
        rest = rest[5:]
    else:
        *acc_ins, _, pack_ref, grad_ref = rest[:7]
        rest = rest[7:]
    (acc_gu, acc_down, acc_head, acc_small, w_gu_ref, normed_s, xhat_s, rstd_s, gate_up_s, hidden_s,
     updated_s, grad_s, gu_grad_s, codes_s, half_grad_s, grad_t_s) = rest
    accs = (acc_gu, acc_down, acc_head, acc_small)

    @pl.when(turn == 0)
    def _():
        w_gu_ref[:, :FF] = w_gate_ref[...]
        w_gu_ref[:, FF:] = w_up_ref[...]
        for n, acc in enumerate(accs):
            acc[...] = jnp.zeros(acc.shape, F32) if first else acc_ins[n][...]

    gain, bias = gain_ref[...], bias_ref[...]
    head_bias = jnp.concatenate([head_bias_ref[...], head_bias_ref[...]], axis=1)
    head_bias = jnp.broadcast_to(head_bias, (128, 128)).T[:NB, :1]

    def forward(n, _):
        at = pl.ds(pl.multiple_of(n * SUB, SUB), SUB)
        rows = pair_ref[pl.ds(n * ROWS, ROWS)].reshape(SUB, C).astype(F32)
        xhat, rstd, normed = normalize(rows, gain, bias)
        normed_s[at, :] = normed
        xhat_s[at, :] = xhat
        rstd_s[at, :] = jnp.broadcast_to(rstd, (SUB, C))
        gate_up = jnp.dot(normed, w_gu_ref[...], preferred_element_type=F32)
        gate_up_s[at, :] = gate_up
        gate, up = gate_up[:, :FF], gate_up[:, FF:]
        hidden = (gate * sigmoid(gate) * up).astype(BF16)
        hidden_s[at, :] = hidden
        updated_s[at, :] = (
            rows + jnp.dot(hidden, w_down_ref[...], preferred_element_type=F32)
        ).astype(BF16)
        return 0

    lax.fori_loop(0, STEPS, forward, 0)

    updated = updated_s[...]
    half = (dot(head_t_ref[...], updated, 1, 1) + head_bias).astype(BF16).astype(F32)
    wire = jnp.where(turn == 0, wire_a_ref[...].astype(F32), wire_b_ref[...].astype(F32))
    mirror = wire[: PAIRS // 2].T
    symmetric = half + jnp.concatenate([mirror[:NB], mirror[NB:]], axis=1)
    symmetric = symmetric - jnp.max(symmetric, axis=0, keepdims=True)
    exped = jnp.exp(symmetric)
    prob = exped / jnp.sum(exped, axis=0, keepdims=True)
    shift = lax.rem(128 - k_ref[turn] * SIDE, 128)
    codes_s[pl.ds(0, SIDE), :] = targets_ref[...].astype(F32)
    codes_s[pl.ds(SIDE, SIDE), :] = mask_ref[...].astype(F32)
    theirs = wire[PAIRS // 2 :]

    def line(rows):
        return jnp.concatenate([rows[r : r + 1] for r in range(8)], axis=1)

    own_target = line(spread(codes_s, 0, shift))
    own_mask = line(spread(codes_s, SIDE, shift))
    their_target, their_mask = line(theirs[:8]), line(theirs[8:])
    level = lax.broadcasted_iota(jnp.int32, (NB, PAIRS), 0).astype(F32)
    half_grad = (
        own_mask * (prob - jnp.where(level == own_target, 1.0, 0.0))
        + their_mask * (prob - jnp.where(level == their_target, 1.0, 0.0))
    ).astype(BF16)
    half_grad_s[...] = half_grad
    head_bias_sum = jnp.sum(half_grad.astype(F32), axis=1, keepdims=True)
    grad_s[...] = dot(half_grad, head_t_ref[...], 0, 0)
    grad_t = dot(head_t_ref[...], half_grad, 0, 0).astype(BF16)
    grad_t_s[...] = grad_t

    def backward(n, carry):
        gain_sum, bias_sum = carry
        at = pl.ds(pl.multiple_of(n * SUB, SUB), SUB)
        grad_in = grad_s[at, :]
        hidden_grad = dot(grad_in.astype(BF16), w_down_ref[...], 1, 1)
        gate, up = gate_up_s[at, :FF], gate_up_s[at, FF:]
        sigma = sigmoid(gate)
        silu = gate * sigma
        gate_grad = (hidden_grad * up * (sigma * (1.0 + gate * (1.0 - sigma)))).astype(BF16)
        up_grad = (hidden_grad * silu).astype(BF16)
        gu_grad_s[at, :FF] = gate_grad
        gu_grad_s[at, FF:] = up_grad
        normed_grad = dot(gu_grad_s[at, :], w_gu_ref[...], 1, 1)
        xhat, rstd = xhat_s[at, :], rstd_s[at, :]
        product = normed_grad * xhat
        gain_sum = gain_sum + jnp.sum(product, axis=0, keepdims=True)
        bias_sum = bias_sum + jnp.sum(normed_grad, axis=0, keepdims=True)
        scaled = normed_grad * gain
        back = rstd * (
            scaled
            - jnp.mean(scaled, axis=-1, keepdims=True)
            - xhat * jnp.mean(product * gain, axis=-1, keepdims=True)
        )
        grad_ref[pl.ds(n * ROWS, ROWS)] = (grad_in + back).astype(BF16).reshape(ROWS, SIDE, C)
        return gain_sum, bias_sum

    gain_sum, bias_sum = lax.fori_loop(
        0, STEPS, backward, (jnp.zeros((1, C), F32), jnp.zeros((1, C), F32))
    )
    head_sum = jnp.dot(half_grad_s[...], updated_s[...], preferred_element_type=F32)
    down_sum = jnp.dot(grad_t_s[...], hidden_s[...], preferred_element_type=F32)
    gu_sum = dot(normed_s[...], gu_grad_s[...], 0, 0)
    head_bias_row = jnp.concatenate(
        [jnp.broadcast_to(head_bias_sum, (NB, 128)), jnp.zeros((NB, 128), F32)], axis=0
    ).T[:1]
    small = jnp.concatenate([gain_sum, bias_sum, head_bias_row, jnp.zeros((5, 128), F32)], axis=0)
    acc_gu[...] += gu_sum
    acc_down[...] += down_sum
    acc_head[...] += head_sum
    acc_small[...] += small

    @pl.when(turn == 1)
    def _():
        if first:
            for acc, out in zip(accs, acc_outs):
                out[...] = acc[...]
        else:
            for b in range(8):
                pack_ref[pl.ds(b * 128, 128), :] = acc_gu[:, b * 128 : b * 128 + 128].astype(BF16)
            for b in range(4):
                pack_ref[pl.ds(1024 + b * 128, 128), :] = acc_down[
                    :, b * 128 : b * 128 + 128
                ].astype(BF16)
            pack_ref[pl.ds(1536, NB), :] = acc_head[...].astype(BF16)
            tail = jnp.concatenate([acc_small[...], jnp.zeros((PACK - 1608, 128), F32)], axis=0)
            pack_ref[pl.ds(1600, PACK - 1600), :] = tail.astype(BF16)


def unpack_kernel(scale, pack_ref, gain_ref, bias_ref, gate_ref, up_ref, down_ref, head_ref, head_bias_ref):
    def block(b):
        return pack_ref[pl.ds(b * 128, 128), :].astype(F32) * scale

    for b in range(4):
        gate_ref[:, b * 128 : b * 128 + 128] = block(b)
        up_ref[:, b * 128 : b * 128 + 128] = block(4 + b)
        down_ref[pl.ds(b * 128, 128), :] = block(8 + b).T
    tail = block(12)
    head_ref[...] = tail[:NB]
    gain_ref[...] = tail[NB : NB + 1]
    bias_ref[...] = tail[NB + 1 : NB + 2]
    head_bias_ref[...] = tail[NB + 2 : NB + 3, :NB]


def full(shape):
    return pl.BlockSpec(shape, lambda i, k: (0,) * len(shape))


def on_device(
    pair, norm_gain, norm_bias, w_gate, w_up, w_down, head_weight, head_bias, targets, mask
):
    length = SIDE * 16
    place = lax.axis_index("x")
    params = pltpu.CompilerParams(vmem_limit_bytes=VMEM_LIMIT)
    common = (
        pair, norm_gain[None], norm_bias[None], w_gate, w_up, w_down, head_weight.T, head_bias[None],
        targets, mask,
    )
    block = pl.BlockSpec((SIDE, SIDE, C), lambda i, k: (0, k[i], 0))
    common_specs = [block] + [full(a.shape) for a in common[1:]]

    def send(shift, blocks):
        wires = pl.pallas_call(
            send_kernel,
            grid_spec=pltpu.PrefetchScalarGridSpec(
                num_scalar_prefetch=1,
                grid=(2,),
                in_specs=common_specs,
                out_specs=[full((WIRE, 128))] * 2,
                scratch_shapes=[
                    pltpu.VMEM((C, 2 * FF), BF16),
                    pltpu.VMEM((PAIRS, 128), F32),
                    pltpu.VMEM((128, 128), F32),
                ],
            ),
            out_shape=[jax.ShapeDtypeStruct((WIRE, 128), BF16)] * 2,
            compiler_params=params,
            name="forward_send",
        )(blocks, *common)
        routes = [
            [
                ((a * 4 + x) * 4 + b, (b * 4 + (x + shift + n) % 4) * 4 + a)
                for a in range(4) for x in range(4) for b in range(4)
            ]
            for n in range(2)
        ]
        return wires, [lax.ppermute(wire, GRID_AXES, route) for wire, route in zip(wires, routes)]

    near = lax.rem(place + jnp.arange(4, dtype=jnp.int32), 4)
    early, wires = send(0, near[:2])
    later, _ = lax.optimization_barrier((near[2:], early))
    wires = wires + send(2, later)[1]
    sums = [
        jax.ShapeDtypeStruct((C, 2 * FF), F32),
        jax.ShapeDtypeStruct((C, FF), F32),
        jax.ShapeDtypeStruct((NB, C), F32),
        jax.ShapeDtypeStruct((8, C), F32),
    ]
    sum_specs = [full(a.shape) for a in sums]
    state = ()
    for first in (True, False):
        shift = 0 if first else 2
        out_shape = sums if first else [jax.ShapeDtypeStruct((PACK, 128), BF16)]
        out_specs = [full(a.shape) for a in out_shape]
        state = pl.pallas_call(
            functools.partial(back_kernel, first),
            grid_spec=pltpu.PrefetchScalarGridSpec(
                num_scalar_prefetch=1,
                grid=(2,),
                in_specs=common_specs
                + [full((WIRE, 128))] * 2
                + ([] if first else sum_specs + [pl.BlockSpec(memory_space=pl.ANY)]),
                out_specs=out_specs + [block],
                scratch_shapes=[pltpu.VMEM(a.shape, F32) for a in sums]
                + [
                    pltpu.VMEM((C, 2 * FF), BF16),
                    pltpu.VMEM((PAIRS, C), BF16),
                    pltpu.VMEM((PAIRS, C), F32),
                    pltpu.VMEM((PAIRS, C), F32),
                    pltpu.VMEM((PAIRS, 2 * FF), F32),
                    pltpu.VMEM((PAIRS, FF), BF16),
                    pltpu.VMEM((PAIRS, C), BF16),
                    pltpu.VMEM((PAIRS, C), F32),
                    pltpu.VMEM((PAIRS, 2 * FF), BF16),
                    pltpu.VMEM((2 * SIDE, 128), F32),
                    pltpu.VMEM((NB, PAIRS), BF16),
                    pltpu.VMEM((C, PAIRS), BF16),
                ],
            ),
            out_shape=out_shape + [jax.ShapeDtypeStruct(pair.shape, BF16)],
            input_output_aliases={} if first else {17: 1},
            compiler_params=params,
            name="backward_blocks",
        )(
            lax.rem(place + 4 - shift - jnp.arange(2, dtype=jnp.int32), 4), *common,
            wires[shift], wires[shift + 1], *state,
        )
    pack, pair_grad = state

    spread_out = lax.all_to_all(pack.reshape(GROUP, SHARE, 128), ("z_lo", "x"), 0, 0)
    share = jnp.sum(spread_out.astype(F32), axis=0).astype(BF16)
    shares = lax.all_gather(share, "z_hi")
    share = jnp.sum(shares.astype(F32), axis=0).astype(BF16)
    pack = lax.all_to_all(
        jnp.broadcast_to(share, (GROUP, SHARE, 128)), ("z_lo", "x"), 0, 0
    ).reshape(PACK, 128)

    outs = pl.pallas_call(
        functools.partial(unpack_kernel, 1.0 / length),
        out_shape=[
            jax.ShapeDtypeStruct((1, C), F32),
            jax.ShapeDtypeStruct((1, C), F32),
            jax.ShapeDtypeStruct((C, FF), F32),
            jax.ShapeDtypeStruct((C, FF), F32),
            jax.ShapeDtypeStruct((FF, C), F32),
            jax.ShapeDtypeStruct((NB, C), F32),
            jax.ShapeDtypeStruct((1, NB), F32),
        ],
        compiler_params=params,
        name="unpack_sums",
    )(pack)
    gain_tot, bias_tot, gate_tot, up_tot, down_tot, head_tot, head_bias_tot = outs
    return (
        pair_grad, gain_tot[0], bias_tot[0], gate_tot, up_tot, down_tot, head_tot.T,
        head_bias_tot[0],
    )


def solution(mesh):
    fine = Mesh(mesh.devices.reshape(8, 4, 4, 4), ("crop",) + GRID_AXES)
    rows = ("crop", "z_lo", "x")
    in_specs = (
        P(rows, "z_hi", None), P(), P(), P(), P(), P(), P("crop", None), P(),
        P(rows, "z_hi"), P(rows, "z_hi"),
    )
    out_specs = (
        P(rows, "z_hi", None), P("crop"), P("crop"), P("crop", None), P("crop", None),
        P("crop", None), P("crop", None), P("crop"),
    )
    return jax.shard_map(
        on_device, mesh=fine, in_specs=in_specs, out_specs=out_specs, check_vma=False
    )
```

```python
import functools

import jax
import jax.numpy as jnp
from jax import lax
from jax.experimental import pallas as pl
from jax.experimental.pallas import tpu as pltpu
from jax.sharding import Mesh, PartitionSpec as P

F32 = jnp.float32
BF16 = jnp.bfloat16
C = 128
FF = 512
NB = 64
SIDE = 32
PAIRS = SIDE * SIDE
SUB = PAIRS
STEPS = PAIRS // SUB
ROWS = SUB // SIDE
WIRE = PAIRS // 2 + 16
GROUP = 16
SHARE = 104
PACK = GROUP * SHARE
GRID_AXES = ("z_lo", "x", "z_hi")
VMEM_ALONE = 60 * 1024 * 1024
VMEM_LIMIT = 36 * 1024 * 1024


def dot(a, b, a_dim, b_dim):
    return lax.dot_general(
        a, b, (((a_dim,), (b_dim,)), ((), ())), preferred_element_type=F32
    )


def normalize(rows, gain, bias):
    mean = jnp.mean(rows, axis=-1, keepdims=True)
    centered = rows - mean
    variance = jnp.mean(centered * centered, axis=-1, keepdims=True)
    rstd = lax.rsqrt(variance + 1e-05)
    xhat = centered * rstd
    return xhat, rstd, (xhat * gain + bias).astype(BF16)


def sigmoid(v):
    return 0.5 * jnp.tanh(0.5 * v) + 0.5


def spread(ref, start, shift):
    lane = lax.broadcasted_iota(jnp.int32, (8, 128), 1)
    out = jnp.zeros((8, 128), F32)
    for u in range(4):
        rows = ref[pl.ds(start + u, 8, stride=4), :]
        rows = pltpu.roll(rows, lax.rem(shift + 32 * u + 128, 128), 1)
        out = jnp.where((lane >= 32 * u) & (lane < 32 * u + 32), rows, out)
    return out


def send_kernel(
    shift, x_ref, pair_ref, gain_ref, bias_ref, w_gate_ref, w_up_ref, w_down_ref, head_t_ref,
    head_bias_ref, targets_ref, mask_ref, *rest,
):
    wire_refs, (w_gu_ref, half_ref, codes_ref) = rest[:2], rest[2:]
    turn = pl.program_id(0)

    @pl.when(turn == 0)
    def _():
        w_gu_ref[:, :FF] = w_gate_ref[...]
        w_gu_ref[:, FF:] = w_up_ref[...]
        codes = jnp.concatenate(
            [targets_ref[...].astype(F32), mask_ref[...].astype(F32), jnp.zeros((64, 128), F32)],
            axis=0,
        )
        codes_ref[...] = codes.T

    head_twice = jnp.concatenate([head_t_ref[...], head_t_ref[...]], axis=0)
    head_bias = jnp.concatenate([head_bias_ref[...], head_bias_ref[...]], axis=1)
    rows = pair_ref[...].reshape(PAIRS, C).astype(F32)
    _, _, normed = normalize(rows, gain_ref[...], bias_ref[...])
    gate_up = jnp.dot(normed, w_gu_ref[...], preferred_element_type=F32)
    gate, up = gate_up[:, :FF], gate_up[:, FF:]
    hidden = (gate * sigmoid(gate) * up).astype(BF16)
    updated = (rows + jnp.dot(hidden, w_down_ref[...], preferred_element_type=F32)).astype(BF16)
    half_ref[...] = dot(updated, head_twice, 1, 1) + head_bias
    lane = lax.broadcasted_iota(jnp.int32, (SIDE, 128), 1)
    start = pl.multiple_of(lax.rem(x_ref[0] + shift + turn, 4) * SIDE, SIDE)

    def write(wire_ref):
        for j in range(SIDE // 2):
            low = half_ref[pl.ds(j, SIDE, stride=SIDE), :]
            high = half_ref[pl.ds(SIDE // 2 + j, SIDE, stride=SIDE), :]
            wire_ref[pl.ds(j * SIDE, SIDE), :] = jnp.where(lane < NB, low, high).astype(BF16)
        wire_ref[pl.ds(PAIRS // 2, 16), :] = jnp.concatenate(
            [spread(codes_ref, start, 0), spread(codes_ref, start, 96)], axis=0
        ).astype(BF16)

    for n in range(2):
        pl.when(turn == n)(functools.partial(write, wire_refs[n]))


def back_kernel(
    first, shift, x_ref, pair_ref, gain_ref, bias_ref, w_gate_ref, w_up_ref, w_down_ref, head_t_ref,
    head_bias_ref, targets_ref, mask_ref, wire_a_ref, wire_b_ref, *rest,
):
    turn = pl.program_id(0)
    if first:
        *acc_outs, grad_ref = rest[:5]
        rest = rest[5:]
    else:
        *acc_ins, _, pack_ref, grad_ref = rest[:7]
        rest = rest[7:]
    (acc_gu, acc_down, acc_head, acc_small, w_gu_ref, normed_s, xhat_s, rstd_s, gate_up_s, hidden_s,
     updated_s, grad_s, gu_grad_s, codes_s, half_grad_s, grad_t_s, wire_s, sems) = rest
    accs = (acc_gu, acc_down, acc_head, acc_small)
    moves = [(wire_a_ref, wire_s.at[0]), (wire_b_ref, wire_s.at[1])]
    if not first:
        moves += zip(acc_ins, accs)
    copies = [pltpu.make_async_copy(a, b, sems.at[n]) for n, (a, b) in enumerate(moves)]

    @pl.when(turn == 0)
    def _():
        w_gu_ref[:, :FF] = w_gate_ref[...]
        w_gu_ref[:, FF:] = w_up_ref[...]
        for copy in copies:
            copy.start()
        if first:
            for acc in accs:
                acc[...] = jnp.zeros(acc.shape, F32)

    gain, bias = gain_ref[...], bias_ref[...]
    head_bias = jnp.concatenate([head_bias_ref[...], head_bias_ref[...]], axis=1)
    head_bias = jnp.broadcast_to(head_bias, (128, 128)).T[:NB, :1]

    def forward(n, _):
        at = pl.ds(pl.multiple_of(n * SUB, SUB), SUB)
        rows = pair_ref[pl.ds(n * ROWS, ROWS)].reshape(SUB, C).astype(F32)
        xhat, rstd, normed = normalize(rows, gain, bias)
        normed_s[at, :] = normed
        xhat_s[at, :] = xhat
        rstd_s[at, :] = jnp.broadcast_to(rstd, (SUB, C))
        gate_up = jnp.dot(normed, w_gu_ref[...], preferred_element_type=F32)
        gate_up_s[at, :] = gate_up
        gate, up = gate_up[:, :FF], gate_up[:, FF:]
        hidden = (gate * sigmoid(gate) * up).astype(BF16)
        hidden_s[at, :] = hidden
        updated_s[at, :] = (
            rows + jnp.dot(hidden, w_down_ref[...], preferred_element_type=F32)
        ).astype(BF16)
        return 0

    lax.fori_loop(0, STEPS, forward, 0)

    updated = updated_s[...]
    half = (dot(head_t_ref[...], updated, 1, 1) + head_bias).astype(BF16).astype(F32)

    @pl.when(turn == 0)
    def _():
        for copy in copies[:2]:
            copy.wait()

    wire = wire_s[turn].astype(F32)
    mirror = wire[: PAIRS // 2].T
    symmetric = half + jnp.concatenate([mirror[:NB], mirror[NB:]], axis=1)
    symmetric = symmetric - jnp.max(symmetric, axis=0, keepdims=True)
    exped = jnp.exp(symmetric)
    prob = exped / jnp.sum(exped, axis=0, keepdims=True)
    lane_shift = lax.rem(128 - lax.rem(x_ref[0] + 4 - shift - turn, 4) * SIDE, 128)
    codes_s[pl.ds(0, SIDE), :] = targets_ref[...].astype(F32)
    codes_s[pl.ds(SIDE, SIDE), :] = mask_ref[...].astype(F32)
    theirs = wire[PAIRS // 2 :]

    def line(rows):
        return jnp.concatenate([rows[r : r + 1] for r in range(8)], axis=1)

    own_target = line(spread(codes_s, 0, lane_shift))
    own_mask = line(spread(codes_s, SIDE, lane_shift))
    their_target, their_mask = line(theirs[:8]), line(theirs[8:])
    level = lax.broadcasted_iota(jnp.int32, (NB, PAIRS), 0).astype(F32)
    half_grad = (
        own_mask * (prob - jnp.where(level == own_target, 1.0, 0.0))
        + their_mask * (prob - jnp.where(level == their_target, 1.0, 0.0))
    ).astype(BF16)
    half_grad_s[...] = half_grad
    head_bias_sum = jnp.sum(half_grad.astype(F32), axis=1, keepdims=True)
    grad_s[...] = dot(half_grad, head_t_ref[...], 0, 0)
    grad_t = dot(head_t_ref[...], half_grad, 0, 0).astype(BF16)
    grad_t_s[...] = grad_t

    def backward(n, carry):
        gain_sum, bias_sum = carry
        at = pl.ds(pl.multiple_of(n * SUB, SUB), SUB)
        grad_in = grad_s[at, :]
        hidden_grad = dot(grad_in.astype(BF16), w_down_ref[...], 1, 1)
        gate, up = gate_up_s[at, :FF], gate_up_s[at, FF:]
        sigma = sigmoid(gate)
        silu = gate * sigma
        gate_grad = (hidden_grad * up * (sigma * (1.0 + gate * (1.0 - sigma)))).astype(BF16)
        up_grad = (hidden_grad * silu).astype(BF16)
        gu_grad_s[at, :FF] = gate_grad
        gu_grad_s[at, FF:] = up_grad
        normed_grad = dot(gu_grad_s[at, :], w_gu_ref[...], 1, 1)
        xhat, rstd = xhat_s[at, :], rstd_s[at, :]
        product = normed_grad * xhat
        gain_sum = gain_sum + jnp.sum(product, axis=0, keepdims=True)
        bias_sum = bias_sum + jnp.sum(normed_grad, axis=0, keepdims=True)
        scaled = normed_grad * gain
        back = rstd * (
            scaled
            - jnp.mean(scaled, axis=-1, keepdims=True)
            - xhat * jnp.mean(product * gain, axis=-1, keepdims=True)
        )
        grad_ref[pl.ds(n * ROWS, ROWS)] = (grad_in + back).astype(BF16).reshape(ROWS, SIDE, C)
        return gain_sum, bias_sum

    gain_sum, bias_sum = lax.fori_loop(
        0, STEPS, backward, (jnp.zeros((1, C), F32), jnp.zeros((1, C), F32))
    )
    head_sum = jnp.dot(half_grad_s[...], updated_s[...], preferred_element_type=F32)
    down_sum = jnp.dot(grad_t_s[...], hidden_s[...], preferred_element_type=F32)
    gu_sum = dot(normed_s[...], gu_grad_s[...], 0, 0)
    head_bias_row = jnp.concatenate(
        [jnp.broadcast_to(head_bias_sum, (NB, 128)), jnp.zeros((NB, 128), F32)], axis=0
    ).T[:1]
    small = jnp.concatenate([gain_sum, bias_sum, head_bias_row, jnp.zeros((5, 128), F32)], axis=0)
    @pl.when(turn == 0)
    def _():
        for copy in copies[2:]:
            copy.wait()

    acc_gu[...] += gu_sum
    acc_down[...] += down_sum
    acc_head[...] += head_sum
    acc_small[...] += small

    @pl.when(turn == 1)
    def _():
        if first:
            for acc, out in zip(accs, acc_outs):
                out[...] = acc[...]
        else:
            for b in range(8):
                pack_ref[pl.ds(b * 128, 128), :] = acc_gu[:, b * 128 : b * 128 + 128].astype(BF16)
            for b in range(4):
                pack_ref[pl.ds(1024 + b * 128, 128), :] = acc_down[
                    :, b * 128 : b * 128 + 128
                ].astype(BF16)
            pack_ref[pl.ds(1536, NB), :] = acc_head[...].astype(BF16)
            tail = jnp.concatenate([acc_small[...], jnp.zeros((PACK - 1608, 128), F32)], axis=0)
            pack_ref[pl.ds(1600, PACK - 1600), :] = tail.astype(BF16)


def unpack_kernel(scale, pack_ref, gain_ref, bias_ref, gate_ref, up_ref, down_ref, head_ref, head_bias_ref):
    def block(b):
        return pack_ref[pl.ds(b * 128, 128), :].astype(F32) * scale

    for b in range(4):
        gate_ref[:, b * 128 : b * 128 + 128] = block(b)
        up_ref[:, b * 128 : b * 128 + 128] = block(4 + b)
        down_ref[pl.ds(b * 128, 128), :] = block(8 + b).T
    tail = block(12)
    head_ref[...] = tail[:NB]
    gain_ref[...] = tail[NB : NB + 1]
    bias_ref[...] = tail[NB + 1 : NB + 2]
    head_bias_ref[...] = tail[NB + 2 : NB + 3, :NB]


def full(shape):
    return pl.BlockSpec(shape, lambda i, k: (0,) * len(shape))


def on_device(
    pair, norm_gain, norm_bias, w_gate, w_up, w_down, head_weight, head_bias, targets, mask
):
    length = SIDE * 16
    place = lax.axis_index("x")[None]
    params = pltpu.CompilerParams(vmem_limit_bytes=VMEM_LIMIT)
    common = (
        pair, norm_gain[None], norm_bias[None], w_gate, w_up, w_down, head_weight.T, head_bias[None],
        targets, mask,
    )
    rest_specs = [full(a.shape) for a in common[1:]]

    def block(shift, sign):
        return pl.BlockSpec(
            (SIDE, SIDE, C), lambda i, x: (0, lax.rem(x[0] + 4 + sign * (shift + i), 4), 0)
        )

    def send(shift, place):
        wires = pl.pallas_call(
            functools.partial(send_kernel, shift),
            grid_spec=pltpu.PrefetchScalarGridSpec(
                num_scalar_prefetch=1,
                grid=(2,),
                in_specs=[block(shift, 1)] + rest_specs,
                out_specs=[full((WIRE, 128))] * 2,
                scratch_shapes=[
                    pltpu.VMEM((C, 2 * FF), BF16),
                    pltpu.VMEM((PAIRS, 128), F32),
                    pltpu.VMEM((128, 128), F32),
                ],
            ),
            out_shape=[jax.ShapeDtypeStruct((WIRE, 128), BF16)] * 2,
            compiler_params=pltpu.CompilerParams(
                vmem_limit_bytes=VMEM_LIMIT if shift else VMEM_ALONE
            ),
            name="forward_send",
        )(place, *common)
        routes = [
            [
                ((a * 4 + x) * 4 + b, (b * 4 + (x + shift + n) % 4) * 4 + a)
                for a in range(4) for x in range(4) for b in range(4)
            ]
            for n in range(2)
        ]
        return wires, [lax.ppermute(wire, GRID_AXES, route) for wire, route in zip(wires, routes)]

    early, wires = send(0, place)
    later, _ = lax.optimization_barrier((place, early))
    wires = wires + send(2, later)[1]
    sums = [
        jax.ShapeDtypeStruct((C, 2 * FF), F32),
        jax.ShapeDtypeStruct((C, FF), F32),
        jax.ShapeDtypeStruct((NB, C), F32),
        jax.ShapeDtypeStruct((8, C), F32),
    ]
    anywhere = pl.BlockSpec(memory_space=pl.ANY)
    state = ()
    for first in (True, False):
        shift = 0 if first else 2
        out_shape = sums if first else [jax.ShapeDtypeStruct((PACK, 128), BF16)]
        out_specs = [full(a.shape) for a in out_shape]
        state = pl.pallas_call(
            functools.partial(back_kernel, first, shift),
            grid_spec=pltpu.PrefetchScalarGridSpec(
                num_scalar_prefetch=1,
                grid=(2,),
                in_specs=[block(shift, -1)] + rest_specs + [anywhere] * (2 if first else 7),
                out_specs=out_specs + [block(shift, -1)],
                scratch_shapes=[pltpu.VMEM(a.shape, F32) for a in sums]
                + [
                    pltpu.VMEM((C, 2 * FF), BF16),
                    pltpu.VMEM((PAIRS, C), BF16),
                    pltpu.VMEM((PAIRS, C), F32),
                    pltpu.VMEM((PAIRS, C), F32),
                    pltpu.VMEM((PAIRS, 2 * FF), F32),
                    pltpu.VMEM((PAIRS, FF), BF16),
                    pltpu.VMEM((PAIRS, C), BF16),
                    pltpu.VMEM((PAIRS, C), F32),
                    pltpu.VMEM((PAIRS, 2 * FF), BF16),
                    pltpu.VMEM((2 * SIDE, 128), F32),
                    pltpu.VMEM((NB, PAIRS), BF16),
                    pltpu.VMEM((C, PAIRS), BF16),
                    pltpu.VMEM((2, WIRE, 128), BF16),
                    pltpu.SemaphoreType.DMA((6,)),
                ],
            ),
            out_shape=out_shape + [jax.ShapeDtypeStruct(pair.shape, BF16)],
            input_output_aliases={} if first else {17: 1},
            compiler_params=params,
            name="backward_blocks",
        )(
            place, *common, wires[shift], wires[shift + 1], *state,
        )
    pack, pair_grad = state

    spread_out = lax.all_to_all(pack.reshape(GROUP, SHARE, 128), ("z_lo", "x"), 0, 0)
    share = jnp.sum(spread_out.astype(F32), axis=0).astype(BF16)
    shares = lax.all_gather(share, "z_hi")
    share = jnp.sum(shares.astype(F32), axis=0).astype(BF16)
    pack = lax.all_to_all(
        jnp.broadcast_to(share, (GROUP, SHARE, 128)), ("z_lo", "x"), 0, 0
    ).reshape(PACK, 128)

    outs = pl.pallas_call(
        functools.partial(unpack_kernel, 1.0 / length),
        out_shape=[
            jax.ShapeDtypeStruct((1, C), F32),
            jax.ShapeDtypeStruct((1, C), F32),
            jax.ShapeDtypeStruct((C, FF), F32),
            jax.ShapeDtypeStruct((C, FF), F32),
            jax.ShapeDtypeStruct((FF, C), F32),
            jax.ShapeDtypeStruct((NB, C), F32),
            jax.ShapeDtypeStruct((1, NB), F32),
        ],
        compiler_params=params,
        name="unpack_sums",
    )(pack)
    gain_tot, bias_tot, gate_tot, up_tot, down_tot, head_tot, head_bias_tot = outs
    return (
        pair_grad, gain_tot[0], bias_tot[0], gate_tot, up_tot, down_tot, head_tot.T,
        head_bias_tot[0],
    )


def solution(mesh):
    fine = Mesh(mesh.devices.reshape(8, 4, 4, 4), ("crop",) + GRID_AXES)
    rows = ("crop", "z_lo", "x")
    in_specs = (
        P(rows, "z_hi", None), P(), P(), P(), P(), P(), P("crop", None), P(),
        P(rows, "z_hi"), P(rows, "z_hi"),
    )
    out_specs = (
        P(rows, "z_hi", None), P("crop"), P("crop"), P("crop", None), P("crop", None),
        P("crop", None), P("crop", None), P("crop"),
    )
    return jax.shard_map(
        on_device, mesh=fine, in_specs=in_specs, out_specs=out_specs, check_vma=False
    )
```

```python
import functools

import jax
import jax.numpy as jnp
from jax import lax
from jax.experimental import pallas as pl
from jax.experimental.pallas import tpu as pltpu
from jax.sharding import Mesh, PartitionSpec as P

F32 = jnp.float32
BF16 = jnp.bfloat16
C = 128
FF = 512
NB = 64
SIDE = 32
PAIRS = SIDE * SIDE
SUB = PAIRS
STEPS = PAIRS // SUB
ROWS = SUB // SIDE
WIRE = PAIRS // 2 + 16
GROUP = 16
SHARE = 104
PACK = GROUP * SHARE
SENDS = ((0, 1), (1, 1), (2, 2))
BACKS = ((0, 1), (1, 1), (2, 1), (3, 1))
GRID_AXES = ("z_lo", "x", "z_hi")
VMEM_ALONE = 60 * 1024 * 1024
VMEM_LIMIT = 36 * 1024 * 1024


def dot(a, b, a_dim, b_dim):
    return lax.dot_general(
        a, b, (((a_dim,), (b_dim,)), ((), ())), preferred_element_type=F32
    )


def normalize(rows, gain, bias):
    mean = jnp.mean(rows, axis=-1, keepdims=True)
    centered = rows - mean
    variance = jnp.mean(centered * centered, axis=-1, keepdims=True)
    rstd = lax.rsqrt(variance + 1e-05)
    xhat = centered * rstd
    return xhat, rstd, (xhat * gain + bias).astype(BF16)


def sigmoid(v):
    return 0.5 * jnp.tanh(0.5 * v) + 0.5


def spread(ref, start, shift):
    lane = lax.broadcasted_iota(jnp.int32, (8, 128), 1)
    out = jnp.zeros((8, 128), F32)
    for u in range(4):
        rows = ref[pl.ds(start + u, 8, stride=4), :]
        rows = pltpu.roll(rows, lax.rem(shift + 32 * u + 128, 128), 1)
        out = jnp.where((lane >= 32 * u) & (lane < 32 * u + 32), rows, out)
    return out


def send_kernel(
    shift, x_ref, pair_ref, gain_ref, bias_ref, w_gate_ref, w_up_ref, w_down_ref, head_t_ref,
    head_bias_ref, targets_ref, mask_ref, *rest,
):
    *wire_refs, w_gu_ref, half_ref, codes_ref = rest
    turn = pl.program_id(0)

    @pl.when(turn == 0)
    def _():
        w_gu_ref[:, :FF] = w_gate_ref[...]
        w_gu_ref[:, FF:] = w_up_ref[...]
        codes = jnp.concatenate(
            [targets_ref[...].astype(F32), mask_ref[...].astype(F32), jnp.zeros((64, 128), F32)],
            axis=0,
        )
        codes_ref[...] = codes.T

    head_twice = jnp.concatenate([head_t_ref[...], head_t_ref[...]], axis=0)
    head_bias = jnp.concatenate([head_bias_ref[...], head_bias_ref[...]], axis=1)
    rows = pair_ref[...].reshape(PAIRS, C).astype(F32)
    _, _, normed = normalize(rows, gain_ref[...], bias_ref[...])
    gate_up = jnp.dot(normed, w_gu_ref[...], preferred_element_type=F32)
    gate, up = gate_up[:, :FF], gate_up[:, FF:]
    hidden = (gate * sigmoid(gate) * up).astype(BF16)
    updated = (rows + jnp.dot(hidden, w_down_ref[...], preferred_element_type=F32)).astype(BF16)
    half_ref[...] = dot(updated, head_twice, 1, 1) + head_bias
    lane = lax.broadcasted_iota(jnp.int32, (SIDE, 128), 1)
    start = pl.multiple_of(lax.rem(x_ref[0] + shift + turn, 4) * SIDE, SIDE)

    def write(wire_ref):
        for j in range(SIDE // 2):
            low = half_ref[pl.ds(j, SIDE, stride=SIDE), :]
            high = half_ref[pl.ds(SIDE // 2 + j, SIDE, stride=SIDE), :]
            wire_ref[pl.ds(j * SIDE, SIDE), :] = jnp.where(lane < NB, low, high).astype(BF16)
        wire_ref[pl.ds(PAIRS // 2, 16), :] = jnp.concatenate(
            [spread(codes_ref, start, 0), spread(codes_ref, start, 96)], axis=0
        ).astype(BF16)

    for n, wire_ref in enumerate(wire_refs):
        pl.when(turn == n)(functools.partial(write, wire_ref))


def back_kernel(
    shift, count, x_ref, pair_ref, gain_ref, bias_ref, w_gate_ref, w_up_ref, w_down_ref, head_t_ref,
    head_bias_ref, targets_ref, mask_ref, *rest,
):
    turn = pl.program_id(0)
    first, last = shift == 0, shift + count == 4
    wire_refs, rest = rest[:count], rest[count:]
    if not first:
        acc_ins, rest = rest[:4], rest[5:]
    if last:
        pack_ref, rest = rest[0], rest[1:]
    else:
        acc_outs, rest = rest[:4], rest[4:]
    grad_ref, *rest = rest
    (acc_gu, acc_down, acc_head, acc_small, w_gu_ref, normed_s, xhat_s, rstd_s, gate_up_s, hidden_s,
     updated_s, grad_s, gu_grad_s, codes_s, half_grad_s, grad_t_s, wire_s, sems) = rest
    accs = (acc_gu, acc_down, acc_head, acc_small)
    moves = [(wire_ref, wire_s.at[n]) for n, wire_ref in enumerate(wire_refs)]
    if not first:
        moves += zip(acc_ins, accs)
    copies = [pltpu.make_async_copy(a, b, sems.at[n]) for n, (a, b) in enumerate(moves)]

    @pl.when(turn == 0)
    def _():
        w_gu_ref[:, :FF] = w_gate_ref[...]
        w_gu_ref[:, FF:] = w_up_ref[...]
        for copy in copies:
            copy.start()
        if first:
            for acc in accs:
                acc[...] = jnp.zeros(acc.shape, F32)

    gain, bias = gain_ref[...], bias_ref[...]
    head_bias = jnp.concatenate([head_bias_ref[...], head_bias_ref[...]], axis=1)
    head_bias = jnp.broadcast_to(head_bias, (128, 128)).T[:NB, :1]

    def forward(n, _):
        at = pl.ds(pl.multiple_of(n * SUB, SUB), SUB)
        rows = pair_ref[pl.ds(n * ROWS, ROWS)].reshape(SUB, C).astype(F32)
        xhat, rstd, normed = normalize(rows, gain, bias)
        normed_s[at, :] = normed
        xhat_s[at, :] = xhat
        rstd_s[at, :] = jnp.broadcast_to(rstd, (SUB, C))
        gate_up = jnp.dot(normed, w_gu_ref[...], preferred_element_type=F32)
        gate_up_s[at, :] = gate_up
        gate, up = gate_up[:, :FF], gate_up[:, FF:]
        hidden = (gate * sigmoid(gate) * up).astype(BF16)
        hidden_s[at, :] = hidden
        updated_s[at, :] = (
            rows + jnp.dot(hidden, w_down_ref[...], preferred_element_type=F32)
        ).astype(BF16)
        return 0

    lax.fori_loop(0, STEPS, forward, 0)

    updated = updated_s[...]
    half = (dot(head_t_ref[...], updated, 1, 1) + head_bias).astype(BF16).astype(F32)

    @pl.when(turn == 0)
    def _():
        for copy in copies[:count]:
            copy.wait()

    wire = wire_s[turn].astype(F32)
    mirror = wire[: PAIRS // 2].T
    symmetric = half + jnp.concatenate([mirror[:NB], mirror[NB:]], axis=1)
    symmetric = symmetric - jnp.max(symmetric, axis=0, keepdims=True)
    exped = jnp.exp(symmetric)
    prob = exped / jnp.sum(exped, axis=0, keepdims=True)
    lane_shift = lax.rem(128 - lax.rem(x_ref[0] + 4 - shift - turn, 4) * SIDE, 128)
    codes_s[pl.ds(0, SIDE), :] = targets_ref[...].astype(F32)
    codes_s[pl.ds(SIDE, SIDE), :] = mask_ref[...].astype(F32)
    theirs = wire[PAIRS // 2 :]

    def line(rows):
        return jnp.concatenate([rows[r : r + 1] for r in range(8)], axis=1)

    own_target = line(spread(codes_s, 0, lane_shift))
    own_mask = line(spread(codes_s, SIDE, lane_shift))
    their_target, their_mask = line(theirs[:8]), line(theirs[8:])
    level = lax.broadcasted_iota(jnp.int32, (NB, PAIRS), 0).astype(F32)
    half_grad = (
        own_mask * (prob - jnp.where(level == own_target, 1.0, 0.0))
        + their_mask * (prob - jnp.where(level == their_target, 1.0, 0.0))
    ).astype(BF16)
    half_grad_s[...] = half_grad
    head_bias_sum = jnp.sum(half_grad.astype(F32), axis=1, keepdims=True)
    grad_s[...] = dot(half_grad, head_t_ref[...], 0, 0)
    grad_t = dot(head_t_ref[...], half_grad, 0, 0).astype(BF16)
    grad_t_s[...] = grad_t

    def backward(n, carry):
        gain_sum, bias_sum = carry
        at = pl.ds(pl.multiple_of(n * SUB, SUB), SUB)
        grad_in = grad_s[at, :]
        hidden_grad = dot(grad_in.astype(BF16), w_down_ref[...], 1, 1)
        gate, up = gate_up_s[at, :FF], gate_up_s[at, FF:]
        sigma = sigmoid(gate)
        silu = gate * sigma
        gate_grad = (hidden_grad * up * (sigma * (1.0 + gate * (1.0 - sigma)))).astype(BF16)
        up_grad = (hidden_grad * silu).astype(BF16)
        gu_grad_s[at, :FF] = gate_grad
        gu_grad_s[at, FF:] = up_grad
        normed_grad = dot(gu_grad_s[at, :], w_gu_ref[...], 1, 1)
        xhat, rstd = xhat_s[at, :], rstd_s[at, :]
        product = normed_grad * xhat
        gain_sum = gain_sum + jnp.sum(product, axis=0, keepdims=True)
        bias_sum = bias_sum + jnp.sum(normed_grad, axis=0, keepdims=True)
        scaled = normed_grad * gain
        back = rstd * (
            scaled
            - jnp.mean(scaled, axis=-1, keepdims=True)
            - xhat * jnp.mean(product * gain, axis=-1, keepdims=True)
        )
        grad_ref[pl.ds(n * ROWS, ROWS)] = (grad_in + back).astype(BF16).reshape(ROWS, SIDE, C)
        return gain_sum, bias_sum

    gain_sum, bias_sum = lax.fori_loop(
        0, STEPS, backward, (jnp.zeros((1, C), F32), jnp.zeros((1, C), F32))
    )
    head_sum = jnp.dot(half_grad_s[...], updated_s[...], preferred_element_type=F32)
    down_sum = jnp.dot(grad_t_s[...], hidden_s[...], preferred_element_type=F32)
    gu_sum = dot(normed_s[...], gu_grad_s[...], 0, 0)
    head_bias_row = jnp.concatenate(
        [jnp.broadcast_to(head_bias_sum, (NB, 128)), jnp.zeros((NB, 128), F32)], axis=0
    ).T[:1]
    small = jnp.concatenate([gain_sum, bias_sum, head_bias_row, jnp.zeros((5, 128), F32)], axis=0)
    @pl.when(turn == 0)
    def _():
        for copy in copies[count:]:
            copy.wait()

    acc_gu[...] += gu_sum
    acc_down[...] += down_sum
    acc_head[...] += head_sum
    acc_small[...] += small

    @pl.when(turn == count - 1)
    def _():
        if not last:
            for acc, out in zip(accs, acc_outs):
                out[...] = acc[...]
        else:
            for b in range(8):
                pack_ref[pl.ds(b * 128, 128), :] = acc_gu[:, b * 128 : b * 128 + 128].astype(BF16)
            for b in range(4):
                pack_ref[pl.ds(1024 + b * 128, 128), :] = acc_down[
                    :, b * 128 : b * 128 + 128
                ].astype(BF16)
            pack_ref[pl.ds(1536, NB), :] = acc_head[...].astype(BF16)
            tail = jnp.concatenate([acc_small[...], jnp.zeros((PACK - 1608, 128), F32)], axis=0)
            pack_ref[pl.ds(1600, PACK - 1600), :] = tail.astype(BF16)


def unpack_kernel(scale, pack_ref, gain_ref, bias_ref, gate_ref, up_ref, down_ref, head_ref, head_bias_ref):
    def block(b):
        return pack_ref[pl.ds(b * 128, 128), :].astype(F32) * scale

    for b in range(4):
        gate_ref[:, b * 128 : b * 128 + 128] = block(b)
        up_ref[:, b * 128 : b * 128 + 128] = block(4 + b)
        down_ref[pl.ds(b * 128, 128), :] = block(8 + b).T
    tail = block(12)
    head_ref[...] = tail[:NB]
    gain_ref[...] = tail[NB : NB + 1]
    bias_ref[...] = tail[NB + 1 : NB + 2]
    head_bias_ref[...] = tail[NB + 2 : NB + 3, :NB]


def full(shape):
    return pl.BlockSpec(shape, lambda i, k: (0,) * len(shape))


def on_device(
    pair, norm_gain, norm_bias, w_gate, w_up, w_down, head_weight, head_bias, targets, mask
):
    length = SIDE * 16
    place = lax.axis_index("x")[None]
    params = pltpu.CompilerParams(vmem_limit_bytes=VMEM_LIMIT)
    common = (
        pair, norm_gain[None], norm_bias[None], w_gate, w_up, w_down, head_weight.T, head_bias[None],
        targets, mask,
    )
    rest_specs = [full(a.shape) for a in common[1:]]

    def block(shift, sign):
        return pl.BlockSpec(
            (SIDE, SIDE, C), lambda i, x: (0, lax.rem(x[0] + 4 + sign * (shift + i), 4), 0)
        )

    def send(shift, count, place):
        wires = pl.pallas_call(
            functools.partial(send_kernel, shift),
            grid_spec=pltpu.PrefetchScalarGridSpec(
                num_scalar_prefetch=1,
                grid=(count,),
                in_specs=[block(shift, 1)] + rest_specs,
                out_specs=[full((WIRE, 128))] * count,
                scratch_shapes=[
                    pltpu.VMEM((C, 2 * FF), BF16),
                    pltpu.VMEM((PAIRS, 128), F32),
                    pltpu.VMEM((128, 128), F32),
                ],
            ),
            out_shape=[jax.ShapeDtypeStruct((WIRE, 128), BF16)] * count,
            compiler_params=pltpu.CompilerParams(
                vmem_limit_bytes=VMEM_LIMIT if shift else VMEM_ALONE
            ),
            name="forward_send",
        )(place, *common)
        routes = [
            [
                ((a * 4 + x) * 4 + b, (b * 4 + (x + shift + n) % 4) * 4 + a)
                for a in range(4) for x in range(4) for b in range(4)
            ]
            for n in range(count)
        ]
        return wires, [lax.ppermute(wire, GRID_AXES, route) for wire, route in zip(wires, routes)]

    wires, turn = [], place
    for shift, count in SENDS:
        sent, arrived = send(shift, count, turn)
        turn, _ = lax.optimization_barrier((place, sent))
        wires += arrived
    sums = [
        jax.ShapeDtypeStruct((C, 2 * FF), F32),
        jax.ShapeDtypeStruct((C, FF), F32),
        jax.ShapeDtypeStruct((NB, C), F32),
        jax.ShapeDtypeStruct((8, C), F32),
    ]
    anywhere = pl.BlockSpec(memory_space=pl.ANY)
    state = ()
    for shift, count in BACKS:
        first, last = shift == 0, shift + count == 4
        out_shape = sums if not last else [jax.ShapeDtypeStruct((PACK, 128), BF16)]
        out_specs = [full(a.shape) for a in out_shape]
        state = pl.pallas_call(
            functools.partial(back_kernel, shift, count),
            grid_spec=pltpu.PrefetchScalarGridSpec(
                num_scalar_prefetch=1,
                grid=(count,),
                in_specs=[block(shift, -1)]
                + rest_specs
                + [anywhere] * (count if first else count + 5),
                out_specs=out_specs + [block(shift, -1)],
                scratch_shapes=[pltpu.VMEM(a.shape, F32) for a in sums]
                + [
                    pltpu.VMEM((C, 2 * FF), BF16),
                    pltpu.VMEM((PAIRS, C), BF16),
                    pltpu.VMEM((PAIRS, C), F32),
                    pltpu.VMEM((PAIRS, C), F32),
                    pltpu.VMEM((PAIRS, 2 * FF), F32),
                    pltpu.VMEM((PAIRS, FF), BF16),
                    pltpu.VMEM((PAIRS, C), BF16),
                    pltpu.VMEM((PAIRS, C), F32),
                    pltpu.VMEM((PAIRS, 2 * FF), BF16),
                    pltpu.VMEM((2 * SIDE, 128), F32),
                    pltpu.VMEM((NB, PAIRS), BF16),
                    pltpu.VMEM((C, PAIRS), BF16),
                    pltpu.VMEM((count, WIRE, 128), BF16),
                    pltpu.SemaphoreType.DMA((count if first else count + 4,)),
                ],
            ),
            out_shape=out_shape + [jax.ShapeDtypeStruct(pair.shape, BF16)],
            input_output_aliases={} if first else {11 + count + 4: len(out_shape)},
            compiler_params=params,
            name="backward_blocks",
        )(
            place, *common, *wires[shift : shift + count], *state,
        )
    pack, pair_grad = state

    spread_out = lax.all_to_all(pack.reshape(GROUP, SHARE, 128), ("z_lo", "x"), 0, 0)
    share = jnp.sum(spread_out.astype(F32), axis=0).astype(BF16)
    shares = lax.all_gather(share, "z_hi")
    share = jnp.sum(shares.astype(F32), axis=0).astype(BF16)
    pack = lax.all_to_all(
        jnp.broadcast_to(share, (GROUP, SHARE, 128)), ("z_lo", "x"), 0, 0
    ).reshape(PACK, 128)

    outs = pl.pallas_call(
        functools.partial(unpack_kernel, 1.0 / length),
        out_shape=[
            jax.ShapeDtypeStruct((1, C), F32),
            jax.ShapeDtypeStruct((1, C), F32),
            jax.ShapeDtypeStruct((C, FF), F32),
            jax.ShapeDtypeStruct((C, FF), F32),
            jax.ShapeDtypeStruct((FF, C), F32),
            jax.ShapeDtypeStruct((NB, C), F32),
            jax.ShapeDtypeStruct((1, NB), F32),
        ],
        compiler_params=params,
        name="unpack_sums",
    )(pack)
    gain_tot, bias_tot, gate_tot, up_tot, down_tot, head_tot, head_bias_tot = outs
    return (
        pair_grad, gain_tot[0], bias_tot[0], gate_tot, up_tot, down_tot, head_tot.T,
        head_bias_tot[0],
    )


def solution(mesh):
    fine = Mesh(mesh.devices.reshape(8, 4, 4, 4), ("crop",) + GRID_AXES)
    rows = ("crop", "z_lo", "x")
    in_specs = (
        P(rows, "z_hi", None), P(), P(), P(), P(), P(), P("crop", None), P(),
        P(rows, "z_hi"), P(rows, "z_hi"),
    )
    out_specs = (
        P(rows, "z_hi", None), P("crop"), P("crop"), P("crop", None), P("crop", None),
        P("crop", None), P("crop", None), P("crop"),
    )
    return jax.shard_map(
        on_device, mesh=fine, in_specs=in_specs, out_specs=out_specs, check_vma=False
    )
```

```python
import functools

import jax
import jax.numpy as jnp
from jax import lax
from jax.experimental import pallas as pl
from jax.experimental.pallas import tpu as pltpu
from jax.sharding import Mesh, PartitionSpec as P

F32 = jnp.float32
BF16 = jnp.bfloat16
C = 128
FF = 512
NB = 64
SIDE = 32
PAIRS = SIDE * SIDE
SUB = PAIRS
STEPS = PAIRS // SUB
ROWS = SUB // SIDE
WIRE = PAIRS // 2 + 16
GROUP = 16
SHARE = 88
PACK = GROUP * SHARE
SENDS = ((0, 1), (1, 1), (2, 2))
BACKS = ((0, 1), (1, 1), (2, 1), (3, 1))
GRID_AXES = ("z_lo", "x", "z_hi")
VMEM_ALONE = 60 * 1024 * 1024
VMEM_LIMIT = 36 * 1024 * 1024


def dot(a, b, a_dim, b_dim):
    return lax.dot_general(
        a, b, (((a_dim,), (b_dim,)), ((), ())), preferred_element_type=F32
    )


def normalize(rows, gain, bias):
    mean = jnp.mean(rows, axis=-1, keepdims=True)
    centered = rows - mean
    variance = jnp.mean(centered * centered, axis=-1, keepdims=True)
    rstd = lax.rsqrt(variance + 1e-05)
    xhat = centered * rstd
    return xhat, rstd, (xhat * gain + bias).astype(BF16)


def sigmoid(v):
    return 0.5 * jnp.tanh(0.5 * v) + 0.5


def spread(ref, start, shift):
    lane = lax.broadcasted_iota(jnp.int32, (8, 128), 1)
    out = jnp.zeros((8, 128), F32)
    for u in range(4):
        rows = ref[pl.ds(start + u, 8, stride=4), :]
        rows = pltpu.roll(rows, lax.rem(shift + 32 * u + 128, 128), 1)
        out = jnp.where((lane >= 32 * u) & (lane < 32 * u + 32), rows, out)
    return out


def send_kernel(
    shift, x_ref, pair_ref, gain_ref, bias_ref, w_gate_ref, w_up_ref, w_down_ref, head_t_ref,
    head_bias_ref, targets_ref, mask_ref, *rest,
):
    *wire_refs, w_gu_ref, half_ref, codes_ref = rest
    turn = pl.program_id(0)

    @pl.when(turn == 0)
    def _():
        w_gu_ref[:, :FF] = w_gate_ref[...]
        w_gu_ref[:, FF:] = w_up_ref[...]
        codes = jnp.concatenate(
            [targets_ref[...].astype(F32), mask_ref[...].astype(F32), jnp.zeros((64, 128), F32)],
            axis=0,
        )
        codes_ref[...] = codes.T

    head_twice = jnp.concatenate([head_t_ref[...], head_t_ref[...]], axis=0)
    head_bias = jnp.concatenate([head_bias_ref[...], head_bias_ref[...]], axis=1)
    rows = pair_ref[...].reshape(PAIRS, C).astype(F32)
    _, _, normed = normalize(rows, gain_ref[...], bias_ref[...])
    gate_up = jnp.dot(normed, w_gu_ref[...], preferred_element_type=F32)
    gate, up = gate_up[:, :FF], gate_up[:, FF:]
    hidden = (gate * sigmoid(gate) * up).astype(BF16)
    updated = (rows + jnp.dot(hidden, w_down_ref[...], preferred_element_type=F32)).astype(BF16)
    half_ref[...] = dot(updated, head_twice, 1, 1) + head_bias
    lane = lax.broadcasted_iota(jnp.int32, (SIDE, 128), 1)
    start = pl.multiple_of(lax.rem(x_ref[0] + shift + turn, 4) * SIDE, SIDE)

    def write(wire_ref):
        for j in range(SIDE // 2):
            low = half_ref[pl.ds(j, SIDE, stride=SIDE), :]
            high = half_ref[pl.ds(SIDE // 2 + j, SIDE, stride=SIDE), :]
            wire_ref[pl.ds(j * SIDE, SIDE), :] = jnp.where(lane < NB, low, high).astype(BF16)
        wire_ref[pl.ds(PAIRS // 2, 16), :] = jnp.concatenate(
            [spread(codes_ref, start, 0), spread(codes_ref, start, 96)], axis=0
        ).astype(BF16)

    for n, wire_ref in enumerate(wire_refs):
        pl.when(turn == n)(functools.partial(write, wire_ref))


def back_kernel(
    shift, count, x_ref, pair_ref, gain_ref, bias_ref, w_gate_ref, w_up_ref, w_down_ref, head_t_ref,
    head_bias_ref, targets_ref, mask_ref, *rest,
):
    turn = pl.program_id(0)
    first, last = shift == 0, shift + count == 4
    wire_refs, rest = rest[:count], rest[count:]
    if not first:
        acc_ins, rest = rest[:4], rest[5:]
    if last:
        pack_ref, rest = rest[0], rest[1:]
    else:
        acc_outs, rest = rest[:4], rest[4:]
    grad_ref, *rest = rest
    (acc_gu, acc_down, acc_head, acc_small, w_gu_ref, normed_s, xhat_s, rstd_s, gate_up_s, hidden_s,
     updated_s, grad_s, gu_grad_s, codes_s, half_grad_s, wire_s, sems) = rest
    accs = (acc_gu, acc_down, acc_head, acc_small)
    moves = [(wire_ref, wire_s.at[n]) for n, wire_ref in enumerate(wire_refs)]
    if not first:
        moves += zip(acc_ins, accs)
    copies = [pltpu.make_async_copy(a, b, sems.at[n]) for n, (a, b) in enumerate(moves)]

    @pl.when(turn == 0)
    def _():
        w_gu_ref[:, :FF] = w_gate_ref[...]
        w_gu_ref[:, FF:] = w_up_ref[...]
        for copy in copies:
            copy.start()
        if first:
            for acc in accs:
                acc[...] = jnp.zeros(acc.shape, F32)

    gain, bias = gain_ref[...], bias_ref[...]
    head_bias = jnp.concatenate([head_bias_ref[...], head_bias_ref[...]], axis=1)
    head_bias = jnp.broadcast_to(head_bias, (128, 128)).T[:NB, :1]

    def forward(n, _):
        at = pl.ds(pl.multiple_of(n * SUB, SUB), SUB)
        rows = pair_ref[pl.ds(n * ROWS, ROWS)].reshape(SUB, C).astype(F32)
        xhat, rstd, normed = normalize(rows, gain, bias)
        normed_s[at, :] = normed
        xhat_s[at, :] = xhat
        rstd_s[at, :] = jnp.broadcast_to(rstd, (SUB, C))
        gate_up = jnp.dot(normed, w_gu_ref[...], preferred_element_type=F32)
        gate_up_s[at, :] = gate_up
        gate, up = gate_up[:, :FF], gate_up[:, FF:]
        hidden = (gate * sigmoid(gate) * up).astype(BF16)
        hidden_s[at, :] = hidden
        updated_s[at, :] = (
            rows + jnp.dot(hidden, w_down_ref[...], preferred_element_type=F32)
        ).astype(BF16)
        return 0

    lax.fori_loop(0, STEPS, forward, 0)

    updated = updated_s[...]
    half = (dot(head_t_ref[...], updated, 1, 1) + head_bias).astype(BF16).astype(F32)

    @pl.when(turn == 0)
    def _():
        for copy in copies[:count]:
            copy.wait()

    wire = wire_s[turn].astype(F32)
    mirror = wire[: PAIRS // 2].T
    symmetric = half + jnp.concatenate([mirror[:NB], mirror[NB:]], axis=1)
    symmetric = symmetric - jnp.max(symmetric, axis=0, keepdims=True)
    exped = jnp.exp(symmetric)
    prob = exped / jnp.sum(exped, axis=0, keepdims=True)
    lane_shift = lax.rem(128 - lax.rem(x_ref[0] + 4 - shift - turn, 4) * SIDE, 128)
    codes_s[pl.ds(0, SIDE), :] = targets_ref[...].astype(F32)
    codes_s[pl.ds(SIDE, SIDE), :] = mask_ref[...].astype(F32)
    theirs = wire[PAIRS // 2 :]

    def line(rows):
        return jnp.concatenate([rows[r : r + 1] for r in range(8)], axis=1)

    own_target = line(spread(codes_s, 0, lane_shift))
    own_mask = line(spread(codes_s, SIDE, lane_shift))
    their_target, their_mask = line(theirs[:8]), line(theirs[8:])
    level = lax.broadcasted_iota(jnp.int32, (NB, PAIRS), 0).astype(F32)
    half_grad = (
        own_mask * (prob - jnp.where(level == own_target, 1.0, 0.0))
        + their_mask * (prob - jnp.where(level == their_target, 1.0, 0.0))
    ).astype(BF16)
    half_grad_s[...] = half_grad
    head_bias_sum = jnp.sum(half_grad.astype(F32), axis=1, keepdims=True)
    grad_s[...] = dot(half_grad, head_t_ref[...], 0, 0)

    def backward(n, carry):
        gain_sum, bias_sum = carry
        at = pl.ds(pl.multiple_of(n * SUB, SUB), SUB)
        grad_in = grad_s[at, :]
        hidden_grad = dot(grad_in.astype(BF16), w_down_ref[...], 1, 1)
        gate, up = gate_up_s[at, :FF], gate_up_s[at, FF:]
        sigma = sigmoid(gate)
        silu = gate * sigma
        gate_grad = (hidden_grad * up * (sigma * (1.0 + gate * (1.0 - sigma)))).astype(BF16)
        up_grad = (hidden_grad * silu).astype(BF16)
        gu_grad_s[at, :FF] = gate_grad
        gu_grad_s[at, FF:] = up_grad
        normed_grad = dot(gu_grad_s[at, :], w_gu_ref[...], 1, 1)
        xhat, rstd = xhat_s[at, :], rstd_s[at, :]
        product = normed_grad * xhat
        gain_sum = gain_sum + jnp.sum(product, axis=0, keepdims=True)
        bias_sum = bias_sum + jnp.sum(normed_grad, axis=0, keepdims=True)
        scaled = normed_grad * gain
        back = rstd * (
            scaled
            - jnp.mean(scaled, axis=-1, keepdims=True)
            - xhat * jnp.mean(product * gain, axis=-1, keepdims=True)
        )
        grad_ref[pl.ds(n * ROWS, ROWS)] = (grad_in + back).astype(BF16).reshape(ROWS, SIDE, C)
        return gain_sum, bias_sum

    gain_sum, bias_sum = lax.fori_loop(
        0, STEPS, backward, (jnp.zeros((1, C), F32), jnp.zeros((1, C), F32))
    )
    head_sum = jnp.dot(half_grad_s[...], updated_s[...], preferred_element_type=F32)
    down_sum = jnp.dot(half_grad_s[...], hidden_s[...], preferred_element_type=F32)
    gu_sum = dot(normed_s[...], gu_grad_s[...], 0, 0)
    head_bias_row = jnp.concatenate(
        [jnp.broadcast_to(head_bias_sum, (NB, 128)), jnp.zeros((NB, 128), F32)], axis=0
    ).T[:1]
    small = jnp.concatenate([gain_sum, bias_sum, head_bias_row, jnp.zeros((5, 128), F32)], axis=0)
    @pl.when(turn == 0)
    def _():
        for copy in copies[count:]:
            copy.wait()

    acc_gu[...] += gu_sum
    acc_down[...] += down_sum
    acc_head[...] += head_sum
    acc_small[...] += small

    @pl.when(turn == count - 1)
    def _():
        if not last:
            for acc, out in zip(accs, acc_outs):
                out[...] = acc[...]
        else:
            for b in range(8):
                pack_ref[pl.ds(b * 128, 128), :] = acc_gu[:, b * 128 : b * 128 + 128].astype(BF16)
            for b in range(4):
                pack_ref[pl.ds(1024 + b * NB, NB), :] = acc_down[
                    :, b * 128 : b * 128 + 128
                ].astype(BF16)
            pack_ref[pl.ds(1280, NB), :] = acc_head[...].astype(BF16)
            tail = jnp.concatenate([acc_small[...], jnp.zeros((PACK - 1352, 128), F32)], axis=0)
            pack_ref[pl.ds(1344, PACK - 1344), :] = tail.astype(BF16)


def unpack_kernel(
    scale, pack_ref, head_t_ref, gain_ref, bias_ref, gate_ref, up_ref, down_ref, head_ref,
    head_bias_ref,
):
    def block(b):
        return pack_ref[pl.ds(b * 128, 128), :].astype(F32) * scale

    head_t = head_t_ref[...].astype(F32)
    head_t = head_t - jnp.mean(head_t, axis=0, keepdims=True)
    head_high = head_t.astype(BF16)
    head_low = (head_t - head_high.astype(F32)).astype(BF16)
    for b in range(4):
        gate_ref[:, b * 128 : b * 128 + 128] = block(b)
        up_ref[:, b * 128 : b * 128 + 128] = block(4 + b)
        by_bin = pack_ref[pl.ds(1024 + b * NB, NB), :]
        down = dot(by_bin, head_high, 0, 0) + dot(by_bin, head_low, 0, 0)
        down_ref[pl.ds(b * 128, 128), :] = down * scale
    tail = pack_ref[pl.ds(1280, 128), :].astype(F32) * scale
    head_ref[...] = tail[:NB]
    gain_ref[...] = tail[NB : NB + 1]
    bias_ref[...] = tail[NB + 1 : NB + 2]
    head_bias_ref[...] = tail[NB + 2 : NB + 3, :NB]


def full(shape):
    return pl.BlockSpec(shape, lambda i, k: (0,) * len(shape))


def on_device(
    pair, norm_gain, norm_bias, w_gate, w_up, w_down, head_weight, head_bias, targets, mask
):
    length = SIDE * 16
    place = lax.axis_index("x")[None]
    params = pltpu.CompilerParams(vmem_limit_bytes=VMEM_LIMIT)
    common = (
        pair, norm_gain[None], norm_bias[None], w_gate, w_up, w_down, head_weight.T, head_bias[None],
        targets, mask,
    )
    rest_specs = [full(a.shape) for a in common[1:]]

    def block(shift, sign):
        return pl.BlockSpec(
            (SIDE, SIDE, C), lambda i, x: (0, lax.rem(x[0] + 4 + sign * (shift + i), 4), 0)
        )

    def send(shift, count, place):
        wires = pl.pallas_call(
            functools.partial(send_kernel, shift),
            grid_spec=pltpu.PrefetchScalarGridSpec(
                num_scalar_prefetch=1,
                grid=(count,),
                in_specs=[block(shift, 1)] + rest_specs,
                out_specs=[full((WIRE, 128))] * count,
                scratch_shapes=[
                    pltpu.VMEM((C, 2 * FF), BF16),
                    pltpu.VMEM((PAIRS, 128), F32),
                    pltpu.VMEM((128, 128), F32),
                ],
            ),
            out_shape=[jax.ShapeDtypeStruct((WIRE, 128), BF16)] * count,
            compiler_params=pltpu.CompilerParams(
                vmem_limit_bytes=VMEM_LIMIT if shift else VMEM_ALONE
            ),
            name="forward_send",
        )(place, *common)
        routes = [
            [
                ((a * 4 + x) * 4 + b, (b * 4 + (x + shift + n) % 4) * 4 + a)
                for a in range(4) for x in range(4) for b in range(4)
            ]
            for n in range(count)
        ]
        return wires, [lax.ppermute(wire, GRID_AXES, route) for wire, route in zip(wires, routes)]

    wires, turn = [], place
    for shift, count in SENDS:
        sent, arrived = send(shift, count, turn)
        turn, _ = lax.optimization_barrier((place, sent))
        wires += arrived
    sums = [
        jax.ShapeDtypeStruct((C, 2 * FF), F32),
        jax.ShapeDtypeStruct((NB, FF), F32),
        jax.ShapeDtypeStruct((NB, C), F32),
        jax.ShapeDtypeStruct((8, C), F32),
    ]
    anywhere = pl.BlockSpec(memory_space=pl.ANY)
    state = ()
    for shift, count in BACKS:
        first, last = shift == 0, shift + count == 4
        out_shape = sums if not last else [jax.ShapeDtypeStruct((PACK, 128), BF16)]
        out_specs = [full(a.shape) for a in out_shape]
        state = pl.pallas_call(
            functools.partial(back_kernel, shift, count),
            grid_spec=pltpu.PrefetchScalarGridSpec(
                num_scalar_prefetch=1,
                grid=(count,),
                in_specs=[block(shift, -1)]
                + rest_specs
                + [anywhere] * (count if first else count + 5),
                out_specs=out_specs + [block(shift, -1)],
                scratch_shapes=[pltpu.VMEM(a.shape, F32) for a in sums]
                + [
                    pltpu.VMEM((C, 2 * FF), BF16),
                    pltpu.VMEM((PAIRS, C), BF16),
                    pltpu.VMEM((PAIRS, C), F32),
                    pltpu.VMEM((PAIRS, C), F32),
                    pltpu.VMEM((PAIRS, 2 * FF), F32),
                    pltpu.VMEM((PAIRS, FF), BF16),
                    pltpu.VMEM((PAIRS, C), BF16),
                    pltpu.VMEM((PAIRS, C), F32),
                    pltpu.VMEM((PAIRS, 2 * FF), BF16),
                    pltpu.VMEM((2 * SIDE, 128), F32),
                    pltpu.VMEM((NB, PAIRS), BF16),
                    pltpu.VMEM((count, WIRE, 128), BF16),
                    pltpu.SemaphoreType.DMA((count if first else count + 4,)),
                ],
            ),
            out_shape=out_shape + [jax.ShapeDtypeStruct(pair.shape, BF16)],
            input_output_aliases={} if first else {11 + count + 4: len(out_shape)},
            compiler_params=params,
            name="backward_blocks",
        )(
            place, *common, *wires[shift : shift + count], *state,
        )
    pack, pair_grad = state

    spread_out = lax.all_to_all(pack.reshape(GROUP, SHARE, 128), ("z_lo", "x"), 0, 0)
    share = jnp.sum(spread_out.astype(F32), axis=0).astype(BF16)
    shares = lax.all_gather(share, "z_hi")
    share = jnp.sum(shares.astype(F32), axis=0).astype(BF16)
    pack = lax.all_to_all(
        jnp.broadcast_to(share, (GROUP, SHARE, 128)), ("z_lo", "x"), 0, 0
    ).reshape(PACK, 128)

    outs = pl.pallas_call(
        functools.partial(unpack_kernel, 1.0 / length),
        out_shape=[
            jax.ShapeDtypeStruct((1, C), F32),
            jax.ShapeDtypeStruct((1, C), F32),
            jax.ShapeDtypeStruct((C, FF), F32),
            jax.ShapeDtypeStruct((C, FF), F32),
            jax.ShapeDtypeStruct((FF, C), F32),
            jax.ShapeDtypeStruct((NB, C), F32),
            jax.ShapeDtypeStruct((1, NB), F32),
        ],
        compiler_params=params,
        name="unpack_sums",
    )(pack, head_weight.T)
    gain_tot, bias_tot, gate_tot, up_tot, down_tot, head_tot, head_bias_tot = outs
    return (
        pair_grad, gain_tot[0], bias_tot[0], gate_tot, up_tot, down_tot, head_tot.T,
        head_bias_tot[0],
    )


def solution(mesh):
    fine = Mesh(mesh.devices.reshape(8, 4, 4, 4), ("crop",) + GRID_AXES)
    rows = ("crop", "z_lo", "x")
    in_specs = (
        P(rows, "z_hi", None), P(), P(), P(), P(), P(), P("crop", None), P(),
        P(rows, "z_hi"), P(rows, "z_hi"),
    )
    out_specs = (
        P(rows, "z_hi", None), P("crop"), P("crop"), P("crop", None), P("crop", None),
        P("crop", None), P("crop", None), P("crop"),
    )
    return jax.shard_map(
        on_device, mesh=fine, in_specs=in_specs, out_specs=out_specs, check_vma=False
    )
```

```python
import functools

import jax
import jax.numpy as jnp
from jax import lax
from jax.experimental import pallas as pl
from jax.experimental.pallas import tpu as pltpu
from jax.sharding import Mesh, PartitionSpec as P

F32 = jnp.float32
BF16 = jnp.bfloat16
C = 128
FF = 512
NB = 64
SIDE = 32
PAIRS = SIDE * SIDE
SUB = PAIRS
STEPS = PAIRS // SUB
ROWS = SUB // SIDE
WIRE = PAIRS // 2 + 16
GROUP = 16
SHARE = 88
PACK = GROUP * SHARE
SENDS = ((0, 1), (1, 1), (2, 1), (3, 1))
BACKS = ((0, 1), (1, 1), (2, 1), (3, 1))
GRID_AXES = ("z_lo", "x", "z_hi")
VMEM_ALONE = 60 * 1024 * 1024
VMEM_LIMIT = 36 * 1024 * 1024


def dot(a, b, a_dim, b_dim):
    return lax.dot_general(
        a, b, (((a_dim,), (b_dim,)), ((), ())), preferred_element_type=F32
    )


def normalize(rows, gain, bias):
    mean = jnp.mean(rows, axis=-1, keepdims=True)
    centered = rows - mean
    variance = jnp.mean(centered * centered, axis=-1, keepdims=True)
    rstd = lax.rsqrt(variance + 1e-05)
    xhat = centered * rstd
    return xhat, rstd, (xhat * gain + bias).astype(BF16)


def sigmoid(v):
    return 0.5 * jnp.tanh(0.5 * v) + 0.5


def spread(ref, start, shift):
    lane = lax.broadcasted_iota(jnp.int32, (8, 128), 1)
    out = jnp.zeros((8, 128), F32)
    for u in range(4):
        rows = ref[pl.ds(start + u, 8, stride=4), :]
        rows = pltpu.roll(rows, lax.rem(shift + 32 * u + 128, 128), 1)
        out = jnp.where((lane >= 32 * u) & (lane < 32 * u + 32), rows, out)
    return out


def send_kernel(
    shift, x_ref, pair_ref, gain_ref, bias_ref, w_gate_ref, w_up_ref, w_down_ref, head_t_ref,
    head_bias_ref, targets_ref, mask_ref, *rest,
):
    *wire_refs, w_gu_ref, half_ref, codes_ref = rest
    turn = pl.program_id(0)

    @pl.when(turn == 0)
    def _():
        w_gu_ref[:, :FF] = w_gate_ref[...]
        w_gu_ref[:, FF:] = w_up_ref[...]
        codes = jnp.concatenate(
            [targets_ref[...].astype(F32), mask_ref[...].astype(F32), jnp.zeros((64, 128), F32)],
            axis=0,
        )
        codes_ref[...] = codes.T

    head_twice = jnp.concatenate([head_t_ref[...], head_t_ref[...]], axis=0)
    head_bias = jnp.concatenate([head_bias_ref[...], head_bias_ref[...]], axis=1)
    rows = pair_ref[...].reshape(PAIRS, C).astype(F32)
    _, _, normed = normalize(rows, gain_ref[...], bias_ref[...])
    gate_up = jnp.dot(normed, w_gu_ref[...], preferred_element_type=F32)
    gate, up = gate_up[:, :FF], gate_up[:, FF:]
    hidden = (gate * sigmoid(gate) * up).astype(BF16)
    updated = (rows + jnp.dot(hidden, w_down_ref[...], preferred_element_type=F32)).astype(BF16)
    half_ref[...] = dot(updated, head_twice, 1, 1) + head_bias
    lane = lax.broadcasted_iota(jnp.int32, (SIDE, 128), 1)
    start = pl.multiple_of(lax.rem(x_ref[0] + shift + turn, 4) * SIDE, SIDE)

    def write(wire_ref):
        for j in range(SIDE // 2):
            low = half_ref[pl.ds(j, SIDE, stride=SIDE), :]
            high = half_ref[pl.ds(SIDE // 2 + j, SIDE, stride=SIDE), :]
            wire_ref[pl.ds(j * SIDE, SIDE), :] = jnp.where(lane < NB, low, high).astype(BF16)
        wire_ref[pl.ds(PAIRS // 2, 16), :] = jnp.concatenate(
            [spread(codes_ref, start, 0), spread(codes_ref, start, 96)], axis=0
        ).astype(BF16)

    for n, wire_ref in enumerate(wire_refs):
        pl.when(turn == n)(functools.partial(write, wire_ref))


def back_kernel(
    shift, count, x_ref, pair_ref, gain_ref, bias_ref, w_gate_ref, w_up_ref, w_down_ref, head_t_ref,
    head_bias_ref, targets_ref, mask_ref, *rest,
):
    turn = pl.program_id(0)
    first, last = shift == 0, shift + count == 4
    wire_refs, rest = rest[:count], rest[count:]
    if not first:
        acc_ins, rest = rest[:4], rest[5:]
    if last:
        pack_ref, rest = rest[0], rest[1:]
    else:
        acc_outs, rest = rest[:4], rest[4:]
    grad_ref, *rest = rest
    (acc_gu, acc_down, acc_head, acc_small, w_gu_ref, normed_s, xhat_s, rstd_s, gate_up_s, hidden_s,
     updated_s, grad_s, gu_grad_s, codes_s, half_grad_s, wire_s, sems) = rest
    accs = (acc_gu, acc_down, acc_head, acc_small)
    moves = [(wire_ref, wire_s.at[n]) for n, wire_ref in enumerate(wire_refs)]
    if not first:
        moves += zip(acc_ins, accs)
    copies = [pltpu.make_async_copy(a, b, sems.at[n]) for n, (a, b) in enumerate(moves)]

    @pl.when(turn == 0)
    def _():
        w_gu_ref[:, :FF] = w_gate_ref[...]
        w_gu_ref[:, FF:] = w_up_ref[...]
        for copy in copies:
            copy.start()
        if first:
            for acc in accs:
                acc[...] = jnp.zeros(acc.shape, F32)

    gain, bias = gain_ref[...], bias_ref[...]
    head_bias = jnp.concatenate([head_bias_ref[...], head_bias_ref[...]], axis=1)
    head_bias = jnp.broadcast_to(head_bias, (128, 128)).T[:NB, :1]

    def forward(n, _):
        at = pl.ds(pl.multiple_of(n * SUB, SUB), SUB)
        rows = pair_ref[pl.ds(n * ROWS, ROWS)].reshape(SUB, C).astype(F32)
        xhat, rstd, normed = normalize(rows, gain, bias)
        normed_s[at, :] = normed
        xhat_s[at, :] = xhat
        rstd_s[at, :] = jnp.broadcast_to(rstd, (SUB, C))
        gate_up = jnp.dot(normed, w_gu_ref[...], preferred_element_type=F32)
        gate_up_s[at, :] = gate_up
        gate, up = gate_up[:, :FF], gate_up[:, FF:]
        hidden = (gate * sigmoid(gate) * up).astype(BF16)
        hidden_s[at, :] = hidden
        updated_s[at, :] = (
            rows + jnp.dot(hidden, w_down_ref[...], preferred_element_type=F32)
        ).astype(BF16)
        return 0

    lax.fori_loop(0, STEPS, forward, 0)

    updated = updated_s[...]
    half = (dot(head_t_ref[...], updated, 1, 1) + head_bias).astype(BF16).astype(F32)

    @pl.when(turn == 0)
    def _():
        for copy in copies[:count]:
            copy.wait()

    wire = wire_s[turn].astype(F32)
    mirror = wire[: PAIRS // 2].T
    symmetric = half + jnp.concatenate([mirror[:NB], mirror[NB:]], axis=1)
    symmetric = symmetric - jnp.max(symmetric, axis=0, keepdims=True)
    exped = jnp.exp(symmetric)
    prob = exped * (1.0 / jnp.sum(exped, axis=0, keepdims=True))
    lane_shift = lax.rem(128 - lax.rem(x_ref[0] + 4 - shift - turn, 4) * SIDE, 128)
    codes_s[pl.ds(0, SIDE), :] = targets_ref[...].astype(F32)
    codes_s[pl.ds(SIDE, SIDE), :] = mask_ref[...].astype(F32)
    theirs = wire[PAIRS // 2 :]

    def line(rows):
        return jnp.concatenate([rows[r : r + 1] for r in range(8)], axis=1)

    own_target = line(spread(codes_s, 0, lane_shift))
    own_mask = line(spread(codes_s, SIDE, lane_shift))
    their_target, their_mask = line(theirs[:8]), line(theirs[8:])
    level = lax.broadcasted_iota(jnp.int32, (NB, PAIRS), 0).astype(F32)
    half_grad = (
        own_mask * (prob - jnp.where(level == own_target, 1.0, 0.0))
        + their_mask * (prob - jnp.where(level == their_target, 1.0, 0.0))
    ).astype(BF16)
    half_grad_s[...] = half_grad
    head_bias_sum = jnp.sum(half_grad.astype(F32), axis=1, keepdims=True)
    grad_s[...] = dot(half_grad, head_t_ref[...], 0, 0)

    def backward(n, carry):
        gain_sum, bias_sum = carry
        at = pl.ds(pl.multiple_of(n * SUB, SUB), SUB)
        grad_in = grad_s[at, :]
        hidden_grad = dot(grad_in.astype(BF16), w_down_ref[...], 1, 1)
        gate, up = gate_up_s[at, :FF], gate_up_s[at, FF:]
        sigma = sigmoid(gate)
        silu = gate * sigma
        gate_grad = (hidden_grad * up * (sigma * (1.0 + gate * (1.0 - sigma)))).astype(BF16)
        up_grad = (hidden_grad * silu).astype(BF16)
        gu_grad_s[at, :FF] = gate_grad
        gu_grad_s[at, FF:] = up_grad
        normed_grad = dot(gu_grad_s[at, :], w_gu_ref[...], 1, 1)
        xhat, rstd = xhat_s[at, :], rstd_s[at, :]
        product = normed_grad * xhat
        gain_sum = gain_sum + jnp.sum(product, axis=0, keepdims=True)
        bias_sum = bias_sum + jnp.sum(normed_grad, axis=0, keepdims=True)
        scaled = normed_grad * gain
        back = rstd * (
            scaled
            - jnp.mean(scaled, axis=-1, keepdims=True)
            - xhat * jnp.mean(product * gain, axis=-1, keepdims=True)
        )
        grad_ref[pl.ds(n * ROWS, ROWS)] = (grad_in + back).astype(BF16).reshape(ROWS, SIDE, C)
        return gain_sum, bias_sum

    gain_sum, bias_sum = lax.fori_loop(
        0, STEPS, backward, (jnp.zeros((1, C), F32), jnp.zeros((1, C), F32))
    )
    head_sum = jnp.dot(half_grad_s[...], updated_s[...], preferred_element_type=F32)
    down_sum = jnp.dot(half_grad_s[...], hidden_s[...], preferred_element_type=F32)
    gu_sum = dot(normed_s[...], gu_grad_s[...], 0, 0)
    head_bias_row = jnp.concatenate(
        [jnp.broadcast_to(head_bias_sum, (NB, 128)), jnp.zeros((NB, 128), F32)], axis=0
    ).T[:1]
    small = jnp.concatenate([gain_sum, bias_sum, head_bias_row, jnp.zeros((5, 128), F32)], axis=0)
    @pl.when(turn == 0)
    def _():
        for copy in copies[count:]:
            copy.wait()

    acc_gu[...] += gu_sum
    acc_down[...] += down_sum
    acc_head[...] += head_sum
    acc_small[...] += small

    @pl.when(turn == count - 1)
    def _():
        if not last:
            for acc, out in zip(accs, acc_outs):
                out[...] = acc[...]
        else:
            for b in range(8):
                pack_ref[pl.ds(b * 128, 128), :] = acc_gu[:, b * 128 : b * 128 + 128].astype(BF16)
            for b in range(4):
                pack_ref[pl.ds(1024 + b * NB, NB), :] = acc_down[
                    :, b * 128 : b * 128 + 128
                ].astype(BF16)
            pack_ref[pl.ds(1280, NB), :] = acc_head[...].astype(BF16)
            tail = jnp.concatenate([acc_small[...], jnp.zeros((PACK - 1352, 128), F32)], axis=0)
            pack_ref[pl.ds(1344, PACK - 1344), :] = tail.astype(BF16)


def unpack_kernel(
    scale, pack_ref, head_t_ref, gain_ref, bias_ref, gate_ref, up_ref, down_ref, head_ref,
    head_bias_ref,
):
    def block(b):
        return pack_ref[pl.ds(b * 128, 128), :].astype(F32) * scale

    head_t = head_t_ref[...].astype(F32)
    head_t = head_t - jnp.mean(head_t, axis=0, keepdims=True)
    head_high = head_t.astype(BF16)
    head_low = (head_t - head_high.astype(F32)).astype(BF16)
    for b in range(4):
        gate_ref[:, b * 128 : b * 128 + 128] = block(b)
        up_ref[:, b * 128 : b * 128 + 128] = block(4 + b)
        by_bin = pack_ref[pl.ds(1024 + b * NB, NB), :]
        down = dot(by_bin, head_high, 0, 0) + dot(by_bin, head_low, 0, 0)
        down_ref[pl.ds(b * 128, 128), :] = down * scale
    tail = pack_ref[pl.ds(1280, 128), :].astype(F32) * scale
    head_ref[...] = tail[:NB]
    gain_ref[...] = tail[NB : NB + 1]
    bias_ref[...] = tail[NB + 1 : NB + 2]
    head_bias_ref[...] = tail[NB + 2 : NB + 3, :NB]


def full(shape):
    return pl.BlockSpec(shape, lambda i, k: (0,) * len(shape))


def on_device(
    pair, norm_gain, norm_bias, w_gate, w_up, w_down, head_weight, head_bias, targets, mask
):
    length = SIDE * 16
    place = lax.axis_index("x")[None]
    params = pltpu.CompilerParams(vmem_limit_bytes=VMEM_LIMIT)
    common = (
        pair, norm_gain[None], norm_bias[None], w_gate, w_up, w_down, head_weight.T, head_bias[None],
        targets, mask,
    )
    rest_specs = [full(a.shape) for a in common[1:]]

    def block(shift, sign):
        return pl.BlockSpec(
            (SIDE, SIDE, C), lambda i, x: (0, lax.rem(x[0] + 4 + sign * (shift + i), 4), 0)
        )

    def send(shift, count, place):
        wires = pl.pallas_call(
            functools.partial(send_kernel, shift),
            grid_spec=pltpu.PrefetchScalarGridSpec(
                num_scalar_prefetch=1,
                grid=(count,),
                in_specs=[block(shift, 1)] + rest_specs,
                out_specs=[full((WIRE, 128))] * count,
                scratch_shapes=[
                    pltpu.VMEM((C, 2 * FF), BF16),
                    pltpu.VMEM((PAIRS, 128), F32),
                    pltpu.VMEM((128, 128), F32),
                ],
            ),
            out_shape=[jax.ShapeDtypeStruct((WIRE, 128), BF16)] * count,
            compiler_params=pltpu.CompilerParams(
                vmem_limit_bytes=VMEM_LIMIT if shift else VMEM_ALONE
            ),
            name="forward_send",
        )(place, *common)
        routes = [
            [
                ((a * 4 + x) * 4 + b, (b * 4 + (x + shift + n) % 4) * 4 + a)
                for a in range(4) for x in range(4) for b in range(4)
            ]
            for n in range(count)
        ]
        return wires, [lax.ppermute(wire, GRID_AXES, route) for wire, route in zip(wires, routes)]

    wires, turn = [], place
    for shift, count in SENDS:
        sent, arrived = send(shift, count, turn)
        turn, _ = lax.optimization_barrier((place, sent))
        wires += arrived
    sums = [
        jax.ShapeDtypeStruct((C, 2 * FF), F32),
        jax.ShapeDtypeStruct((NB, FF), F32),
        jax.ShapeDtypeStruct((NB, C), F32),
        jax.ShapeDtypeStruct((8, C), F32),
    ]
    anywhere = pl.BlockSpec(memory_space=pl.ANY)
    state = ()
    for shift, count in BACKS:
        first, last = shift == 0, shift + count == 4
        out_shape = sums if not last else [jax.ShapeDtypeStruct((PACK, 128), BF16)]
        out_specs = [full(a.shape) for a in out_shape]
        state = pl.pallas_call(
            functools.partial(back_kernel, shift, count),
            grid_spec=pltpu.PrefetchScalarGridSpec(
                num_scalar_prefetch=1,
                grid=(count,),
                in_specs=[block(shift, -1)]
                + rest_specs
                + [anywhere] * (count if first else count + 5),
                out_specs=out_specs + [block(shift, -1)],
                scratch_shapes=[pltpu.VMEM(a.shape, F32) for a in sums]
                + [
                    pltpu.VMEM((C, 2 * FF), BF16),
                    pltpu.VMEM((PAIRS, C), BF16),
                    pltpu.VMEM((PAIRS, C), F32),
                    pltpu.VMEM((PAIRS, C), F32),
                    pltpu.VMEM((PAIRS, 2 * FF), F32),
                    pltpu.VMEM((PAIRS, FF), BF16),
                    pltpu.VMEM((PAIRS, C), BF16),
                    pltpu.VMEM((PAIRS, C), F32),
                    pltpu.VMEM((PAIRS, 2 * FF), BF16),
                    pltpu.VMEM((2 * SIDE, 128), F32),
                    pltpu.VMEM((NB, PAIRS), BF16),
                    pltpu.VMEM((count, WIRE, 128), BF16),
                    pltpu.SemaphoreType.DMA((count if first else count + 4,)),
                ],
            ),
            out_shape=out_shape + [jax.ShapeDtypeStruct(pair.shape, BF16)],
            input_output_aliases={} if first else {11 + count + 4: len(out_shape)},
            compiler_params=params,
            name="backward_blocks",
        )(
            place, *common, *wires[shift : shift + count], *state,
        )
    pack, pair_grad = state

    spread_out = lax.all_to_all(pack.reshape(GROUP, SHARE, 128), ("z_lo", "x"), 0, 0)
    share = jnp.sum(spread_out.astype(F32), axis=0).astype(BF16)
    shares = lax.all_gather(share, "z_hi")
    share = jnp.sum(shares.astype(F32), axis=0).astype(BF16)
    pack = lax.all_to_all(
        jnp.broadcast_to(share, (GROUP, SHARE, 128)), ("z_lo", "x"), 0, 0
    ).reshape(PACK, 128)

    outs = pl.pallas_call(
        functools.partial(unpack_kernel, 1.0 / length),
        out_shape=[
            jax.ShapeDtypeStruct((1, C), F32),
            jax.ShapeDtypeStruct((1, C), F32),
            jax.ShapeDtypeStruct((C, FF), F32),
            jax.ShapeDtypeStruct((C, FF), F32),
            jax.ShapeDtypeStruct((FF, C), F32),
            jax.ShapeDtypeStruct((NB, C), F32),
            jax.ShapeDtypeStruct((1, NB), F32),
        ],
        compiler_params=params,
        name="unpack_sums",
    )(pack, head_weight.T)
    gain_tot, bias_tot, gate_tot, up_tot, down_tot, head_tot, head_bias_tot = outs
    return (
        pair_grad, gain_tot[0], bias_tot[0], gate_tot, up_tot, down_tot, head_tot.T,
        head_bias_tot[0],
    )


def solution(mesh):
    fine = Mesh(mesh.devices.reshape(8, 4, 4, 4), ("crop",) + GRID_AXES)
    rows = ("crop", "z_lo", "x")
    in_specs = (
        P(rows, "z_hi", None), P(), P(), P(), P(), P(), P("crop", None), P(),
        P(rows, "z_hi"), P(rows, "z_hi"),
    )
    out_specs = (
        P(rows, "z_hi", None), P("crop"), P("crop"), P("crop", None), P("crop", None),
        P("crop", None), P("crop", None), P("crop"),
    )
    return jax.shard_map(
        on_device, mesh=fine, in_specs=in_specs, out_specs=out_specs, check_vma=False
    )
```
